512 devices in a mesh: enc: 32 (over y, x_hi, core), seq: 16 (over z, x_lo).
Axes of the slice: x: 4 (x_hi: 2, x_lo: 2; x = x_hi * 2 + x_lo), y: 8, z: 8, core: 2. Of those that a mesh axis runs over, the one named last changes fastest.
Arguments:
- tile_features: bfloat16 [32, 256, 2560], P('enc', 'seq'), may hold values from -6 to 6
- proj_weight: bfloat16 [2560, 4096], P(None, 'seq'), may hold values from -0.125 to 0.125
- text_embed: bfloat16 [32, 2048, 4096], P('enc', 'seq'), may hold values from -8 to 8
- out_grad: bfloat16 [32, 2048, 4096], P('enc', 'seq'), may hold values from -6 to 6
- score_gain: float32 [4096], P('seq'), may hold values from -6 to 6
- tile_count: int32 [32], P('enc'), may hold values from 0 to 1, as said below
- tile_slot: int32 [32, 1], P('enc'), may hold values from 0 to 7, as said below
- doc_id: int32 [32, 2048], P('enc'), may hold values from 0 to 7, never falling along the last dimension, each value on 1 to 1024 neighbouring positions
Outputs:
- text_grad: bfloat16 [32, 2048, 4096], P('enc', 'seq')
- weight_grad: float32 [2560, 4096], P('enc', 'seq')
The draws below stay inside these ranges and needn't reach their ends.
Inputs may be any that keep to these rules, and one draw needn't show every extreme that they name: `tile_count`: in every draw some sequence has 1 tiles. `tile_slot`: the 1 entries of a sequence are different slots; slot j covers positions j * 256 to j * 256 + 255; only the first tile_count entries are used.
All inputs are finite; a program needn't handle non-finite values.
Results may differ from the reference program's by a relative error of at most 0.013.
The reference program's roundings to bfloat16 on the way count: a program that leaves them out, or rounds other values in their place, can miss the bound.
Values may be sent and summed in bfloat16 or wider, within the bound.
A program may use at most 128 MiB of HBM per device.

```python
import math
import jax
import jax.numpy as jnp
import numpy as np
from jax import lax

D_E = 2560
D = 4096
HEAD = 128
TILE_TOK = 256
DOCS = 8
LENGTH = 2048
SEQS = 32
TILE_MAX = 1
TILE_ROWS = 256
SLOTS = 8


def gain_values(key):
    return jax.random.truncated_normal(key, -4.0, 4.0, (D,), jnp.float32)


def draw_score_gain(key, part):
    values = gain_values(key)
    return values


def draw_text_embed(key, part):
    key = jax.random.fold_in(key, 12)
    base_key = jax.random.fold_in(key, 0)
    dims = (SEQS, LENGTH, D)
    return jax.random.truncated_normal(base_key, -8.0, 8.0, dims, jnp.float32).astype(jnp.bfloat16)


def draw_tile_count(key, part):
    key = jax.random.fold_in(key, 13)
    count_key, pick_key = jax.random.split(key)
    counts = jax.random.randint(count_key, (SEQS,), 0, TILE_MAX + 1)
    fullest = jax.random.randint(pick_key, (), 0, SEQS)
    return counts.at[fullest].set(TILE_MAX).astype(jnp.int32)


def draw_tile_slot(key, part):
    key = jax.random.fold_in(key, 14)
    ranks = jax.random.randint(key, (SEQS, SLOTS), 0, 1 << 20) * SLOTS + jnp.arange(SLOTS, dtype=jnp.int32)
    ordering = jnp.argsort(ranks, axis=1, stable=True)
    return ordering[:, :TILE_MAX].astype(jnp.int32)


def spiked(values, own_key, source, target, blocks, factor):
    def block_of(axis_at):
        return (jnp.arange(values.shape[axis_at]) // (values.shape[axis_at] // blocks)).reshape((-1,) + (1,) * (values.ndim - 1 - axis_at))

    near = jax.random.permutation(own_key, blocks)[block_of(target)]
    far = (block_of(target) + blocks // 2) % blocks
    return jnp.where((block_of(source) == near) | (block_of(source) == far), factor * values, values)


def shard_levels(key, shape, shards, least, top_value):
    level = 1.0
    for dim, parts in shards:
        heights = jax.random.uniform(jax.random.fold_in(jax.random.fold_in(key, 6), dim), (parts,), jnp.float32, least / len(shards), top_value / len(shards))
        level = level * jnp.repeat(jnp.exp(heights), shape[dim] // parts).reshape((-1,) + (1,) * (len(shape) - 1 - dim))
    return level


def split_up(count, total, reach, skew):
    loads = [(1 << 20) // math.isqrt(rank ** skew) + 1 for rank in range(2, count + 1)]
    surplus, holding = total - reach - (count - 1), [1] * (count - 1)
    while surplus > 0:
        free = [i for i in range(count - 1) if holding[i] < reach]
        pool, left = sum([loads[i] for i in free]), surplus
        for i in free:
            more = min(reach - holding[i], max(1, left * loads[i] // pool), surplus)
            holding[i] = holding[i] + more
            surplus = surplus - more
    return np.array([reach] + holding)


def uneven(own_key, count, total, most, slope):
    if count == 2:
        one = jax.random.randint(own_key, (), max(1, total - most), min(most, total - 1) + 1)
        return jnp.stack([one, total - one])
    sizes = jnp.asarray(split_up(count, total, most, slope), jnp.int32)
    couples = (count - 1) // 2
    donor, taker = sizes[1:1 + 2 * couples:2], sizes[2:2 + 2 * couples:2]
    room = jnp.minimum(donor - 1, most - taker)
    shifted = jax.random.randint(jax.random.fold_in(own_key, 1), (couples,), 0, 1 << 20) % (room + 1)
    sizes = sizes.at[1:1 + 2 * couples:2].set(donor - shifted).at[2:2 + 2 * couples:2].set(taker + shifted)
    return sizes[jax.random.permutation(jax.random.fold_in(own_key, 2), count)]


def gaussian(own_key, extent, scale, bound, cuts=(), kind=jnp.bfloat16):
    drawn = scale * jax.random.normal(own_key, extent, jnp.float32)
    if cuts:
        drawn = drawn * shard_levels(own_key, extent, cuts, -0.22, 0.18)
    return jnp.clip(drawn, -bound, bound).astype(kind)


def heavy_noise(rng, shape, scale, reach, pieces, heavy, kind=jnp.bfloat16):
    values = scale * jax.random.normal(rng, shape, jnp.float32)
    if pieces:
        values = values * shard_levels(rng, shape, pieces, -0.22, 0.18)
    return jnp.clip(spiked(values, jax.random.fold_in(rng, 3), *heavy), -reach, reach).astype(kind)


def setup_inputs(seed: int = 0) -> dict:
    seeds = jax.random.split(jax.random.key(seed), 9)
    tile_features = heavy_noise(seeds[0], (SEQS, TILE_ROWS, D_E), 1.0, 6.0, ((0, 32), (1, 16)), (0, 2, 32, 2.75))
    proj_weight = gaussian(seeds[1], (D_E, D), D_E ** -0.5, 0.125, ((1, 16),))
    text_embed = draw_text_embed(jax.random.fold_in(seeds[8], 71), 0)
    out_grad = gaussian(seeds[3], (SEQS, LENGTH, D), 1.0, 6.0, ((0, 32), (1, 16)))
    score_gain = draw_score_gain(jax.random.fold_in(seeds[8], 71), 0)
    tile_count = draw_tile_count(jax.random.fold_in(seeds[8], 71), 0)
    tile_slot = draw_tile_slot(jax.random.fold_in(seeds[8], 71), 0)
    doc_id = jax.vmap(lambda own: jnp.searchsorted(jnp.cumsum(uneven(own, DOCS, LENGTH, LENGTH // 2, 2)), jnp.arange(LENGTH), side="right"))(jax.random.split(seeds[7], SEQS)).reshape((SEQS, LENGTH)).astype(jnp.int32)
    return dict(tile_features=tile_features, proj_weight=proj_weight, text_embed=text_embed, out_grad=out_grad, score_gain=score_gain, tile_count=tile_count, tile_slot=tile_slot, doc_id=doc_id)


def head_grads(emb_head, gain_head, cot_head, doc_row):
    length = emb_head.shape[0]
    scaling = HEAD ** -0.5
    queries = (emb_head.astype(jnp.float32) * gain_head).astype(jnp.bfloat16)
    scores = jnp.dot(queries, emb_head.T, preferred_element_type=jnp.float32) * scaling
    position = jnp.arange(length, dtype=jnp.int32)
    allowed = (position[None, :] <= position[:, None]) & (doc_row[None, :] == doc_row[:, None])
    scores = jnp.where(allowed, scores, jnp.float32(-1e30))
    row_max = jnp.max(scores, axis=1, keepdims=True)
    weights = jnp.where(allowed, jnp.exp(scores - row_max), jnp.float32(0.0))
    prob_rows = weights / jnp.sum(weights, axis=1, keepdims=True)
    prob_low = prob_rows.astype(jnp.bfloat16)
    d_prob = jnp.dot(cot_head, emb_head.T, preferred_element_type=jnp.float32)
    row_term = jnp.sum(prob_rows * d_prob, axis=1, keepdims=True)
    d_scores = (prob_rows * (d_prob - row_term) * scaling).astype(jnp.bfloat16)
    d_query = jnp.dot(d_scores, emb_head, preferred_element_type=jnp.float32)
    d_key = jnp.dot(d_scores.T, queries, preferred_element_type=jnp.float32)
    d_value = jnp.dot(prob_low.T, cot_head, preferred_element_type=jnp.float32)
    return d_query * gain_head + d_key + d_value


def sequence_grads(features, weight, text_rows, cotangent, gains, tile_total, slot_ids, doc_row):
    projected = jnp.dot(features, weight, preferred_element_type=jnp.float32).astype(jnp.bfloat16)
    live_tiles = jnp.arange(TILE_MAX, dtype=jnp.int32) < tile_total
    choose = (slot_ids[None, :] == jnp.arange(SLOTS, dtype=jnp.int32)[:, None]) & live_tiles[None, :]
    choose_low = choose.astype(jnp.bfloat16)
    tile_block = projected.reshape(TILE_MAX, TILE_TOK * D)
    placed = jnp.dot(choose_low, tile_block, preferred_element_type=jnp.float32).astype(jnp.bfloat16).reshape(LENGTH, D)
    is_image = jnp.repeat(jnp.any(choose, axis=1), TILE_TOK)
    embedding = jnp.where(is_image[:, None], placed, text_rows)

    def one_head(head_index):
        offset = head_index * HEAD
        return head_grads(lax.dynamic_slice_in_dim(embedding, offset, HEAD, 1),
                          lax.dynamic_slice_in_dim(gains, offset, HEAD, 0),
                          lax.dynamic_slice_in_dim(cotangent, offset, HEAD, 1), doc_row)

    per_head = lax.map(one_head, jnp.arange(D // HEAD, dtype=jnp.int32))
    gradient = jnp.transpose(per_head, (1, 0, 2)).reshape(LENGTH, D)
    grad_low = gradient.astype(jnp.bfloat16)
    text_grad = jnp.where(is_image[:, None], jnp.zeros_like(grad_low), grad_low)
    image_grad = jnp.dot(choose_low.T, grad_low.reshape(SLOTS, TILE_TOK * D),
                         preferred_element_type=jnp.float32).astype(jnp.bfloat16).reshape(TILE_ROWS, D)
    weight_term = jnp.dot(features.T, image_grad, preferred_element_type=jnp.float32)
    return text_grad, weight_term


def reference(tile_features, proj_weight, text_embed, out_grad, score_gain, tile_count, tile_slot, doc_id):
    def per_sequence(accumulated, inputs):
        features, text_rows, cotangent, tile_total, slot_ids, doc_row = inputs
        text_grad, weight_term = sequence_grads(features, proj_weight, text_rows, cotangent, score_gain,
                                                tile_total, slot_ids, doc_row)
        return accumulated + weight_term, text_grad

    accumulated, text_grad = lax.scan(per_sequence, jnp.zeros((D_E, D), jnp.float32),
                                      (tile_features, text_embed, out_grad, tile_count, tile_slot, doc_id))
    return text_grad, accumulated * (1.0 / TILE_TOK)
```

```python
import functools

import jax
import jax.numpy as jnp
from jax import lax
from jax.experimental import pallas as pl
from jax.experimental.pallas import tpu as pltpu
from jax.sharding import PartitionSpec as P

HEAD = 128
TILE_TOK = 256
BLOCK = 128
REACH = 1024
DOC_VALUES = 8
NEG = -1e30
MESH = pl.DeviceIdType.MESH
F32 = jnp.float32
BF16 = jnp.bfloat16


def whole_kernel(
    n,
    heads,
    enc,
    feat,
    weight,
    text,
    cot,
    gain,
    count,
    slot,
    doc,
    out,
    wgrad,
    features,
    featT,
    wv,
    projected,
    tx,
    qc,
    emb,
    embT,
    dkv,
    pair,
    image,
    send_block,
    first,
    keep,
    half_out,
    half_in,
    sum_out,
    sum_in,
    local_sem,
    gather_send,
    gather_recv,
    in_send,
    in_recv,
    grad_send,
    grad_recv,
    half_send,
    half_recv,
    sum_send,
    sum_recv,
    block_sem,
):
    me = lax.axis_index("seq")
    my_enc = lax.axis_index("enc")
    core = lax.rem(my_enc, 2)
    chip = lax.div(my_enc, 2)
    chips = enc // 2
    other_core = my_enc + 1 - 2 * core
    beside = me + 1 - 2 * lax.rem(me, 2)
    columns = heads * HEAD
    shard = feat.shape[1]
    depth = feat.shape[2]
    length = n * BLOCK
    out_rows = depth // enc
    peers = n - 1

    def seq_id(index):
        return (my_enc, index)

    def along(step):
        return lax.rem(me + 2 * step + 2 * n, n)

    def rows(index, size):
        return pl.ds(pl.multiple_of(index * size, size), size)

    weight_copy = pltpu.make_async_copy(weight, wv, local_sem.at[0])
    weight_copy.start()
    own_features = pltpu.make_async_copy(
        feat.at[0], features.at[rows(me, shard)], local_sem.at[1]
    )
    own_features.start()
    own = []
    for h in range(heads):
        cols = pl.ds(pl.multiple_of(me * columns + h * HEAD, HEAD), HEAD)
        own.append(
            pltpu.make_async_copy(
                text.at[0, :, cols], tx.at[h, rows(me, BLOCK)], local_sem.at[2 + 2 * h]
            )
        )
        own.append(
            pltpu.make_async_copy(
                cot.at[0, :, cols],
                qc.at[h, me, pl.ds(BLOCK, BLOCK)],
                local_sem.at[3 + 2 * h],
            )
        )
    for copy in own:
        copy.start()

    barrier = pltpu.get_barrier_semaphore()

    def greet_seq(d, carry):
        pl.semaphore_signal(
            barrier, inc=1, device_id=seq_id(lax.rem(me + d, n)), device_id_type=MESH
        )
        return carry

    def greet_enc(d, carry):
        to = 2 * lax.rem(chip + d, chips) + core
        pl.semaphore_signal(barrier, inc=1, device_id=(to, me), device_id_type=MESH)
        return carry

    lax.fori_loop(1, n, greet_seq, 0)
    lax.fori_loop(1, chips, greet_enc, 0)
    pl.semaphore_signal(barrier, inc=1, device_id=(other_core, me), device_id_type=MESH)
    pl.semaphore_wait(barrier, peers + chips)

    def pass_on(source, index, to, number, first_col=0, cols=depth):
        span = pl.ds(first_col, cols)
        place = features.at[rows(index, shard), span]
        return pltpu.make_async_remote_copy(
            src_ref=place if source is None else source,
            dst_ref=place,
            send_sem=gather_send.at[number],
            recv_sem=gather_recv.at[number],
            device_id=seq_id(to),
            device_id_type=MESH,
        )

    ring = n // 2
    ahead, behind = along(1), along(-1)
    full_steps = ring // 2 - 1
    half = depth // 2

    def exchange(h, source, to_cot, begin, end):
        def body(d, carry):
            to = lax.rem(me + d, n)
            cols = pl.ds(pl.multiple_of(to * columns + h * HEAD, HEAD), HEAD)
            if to_cot:
                place = qc.at[h, me, pl.ds(BLOCK, BLOCK)]
            else:
                place = tx.at[h, rows(me, BLOCK)]
            pltpu.make_async_remote_copy(
                src_ref=source.at[0, :, cols],
                dst_ref=place,
                send_sem=in_send.at[2 * h + to_cot],
                recv_sem=in_recv.at[2 * h + to_cot],
                device_id=seq_id(to),
                device_id_type=MESH,
            ).start()
            return carry

        lax.fori_loop(begin, end, body, 0)

    def exchange_part(h, part, parts):
        begin = 1 + peers * part // parts
        end = 1 + peers * (part + 1) // parts
        exchange(h, text, 0, begin, end)
        exchange(h, cot, 1, begin, end)

    x_base = 2 * (full_steps + 1)
    copies = []
    parts = full_steps + 1
    for step in range(full_steps):
        if step == 0:
            source = feat.at[0]
            right = pass_on(source, me, ahead, 0)
            left = pass_on(source, me, behind, full_steps + 1)
            sideways = [pass_on(source, me, beside, x_base)]
        else:
            copies[-1][0].wait_recv()
            right = pass_on(None, along(-step), ahead, step)
            copies[-1][1].wait_recv()
            left = pass_on(None, along(step), behind, full_steps + 1 + step)
            sideways = [
                pass_on(None, along(-step), beside, x_base + 2 * step - 1),
                pass_on(None, along(step), beside, x_base + 2 * step),
            ]
        for copy in [right, left] + sideways:
            copy.start()
        copies.append([right, left] + sideways)
        exchange_part(0, step, parts)
    copies[-1][0].wait_recv()
    copies[-1][1].wait_recv()
    last = full_steps
    right = pass_on(None, along(-last), ahead, last, 0, half)
    left = pass_on(None, along(last), behind, full_steps + 1 + last, half, half)
    sideways = [
        pass_on(None, along(-last), beside, x_base + 2 * last - 1),
        pass_on(None, along(last), beside, x_base + 2 * last),
    ]
    for copy in [right, left] + sideways:
        copy.start()
    exchange_part(0, parts - 1, parts)
    right.wait_recv()
    left.wait_recv()
    farthest = pass_on(None, along(ring // 2), beside, x_base + 2 * last + 1)
    farthest.start()
    copies.append([right, left] + sideways + [farthest])

    for h in range(1, heads):
        exchange_part(h, 0, 1)

    doc_row = doc[...]
    begins = jnp.zeros_like(doc_row)
    for value in range(1, DOC_VALUES):
        below = jnp.sum((doc_row < value).astype(jnp.int32), axis=1, keepdims=True)
        begins = jnp.where(doc_row >= value, below, begins)
    first[...] = begins
    tile = jnp.where(count[0] > 0, slot[0, 0], -1)

    for group in copies:
        for copy in group[2:]:
            copy.wait_recv()
    own_features.wait()
    weight_copy.wait()

    projected[...] = jnp.dot(
        features[...], wv[...], preferred_element_type=F32
    ).astype(BF16)

    def turn_features(index, carry):
        place = rows(index, HEAD)
        featT[place, :] = features[:, place].T
        return carry

    lax.fori_loop(0, depth // HEAD, turn_features, 0)
    for copy in own:
        copy.wait()

    scaling = HEAD ** (-0.5)
    log2_scaling = scaling * 1.4426950408889634
    tile_blocks = TILE_TOK // BLOCK

    def of_tile(block):
        return jnp.full((BLOCK, HEAD), tile, jnp.int32) == lax.div(block, tile_blocks)

    def await_blocks(like, sem):
        pltpu.make_async_copy(like, like, sem).wait()

    def one_head(h, head_carry):
        head_cols = rows(h, HEAD)
        gain_row = gain[:, head_cols]
        arrived = tx.at[h, pl.ds(0, peers * BLOCK)]
        await_blocks(arrived, in_recv.at[2 * h])
        await_blocks(arrived, in_recv.at[2 * h + 1])

        def prepare(block, carry):
            place = rows(block, BLOCK)
            part = rows(lax.rem(block, tile_blocks), BLOCK)
            value = jnp.where(
                of_tile(block),
                projected[part, head_cols].astype(F32),
                tx[h, place, :].astype(F32),
            )
            low = value.astype(BF16)
            emb[place, :] = low
            embT[:, place] = value.T.astype(BF16)
            qc[h, block, 0:BLOCK, :] = (value * gain_row).astype(BF16)
            return carry

        lax.fori_loop(0, n, prepare, 0)
        dkv[...] = jnp.zeros_like(dkv)
        image[...] = jnp.zeros_like(image)

        def attend(block, base, width, plain):
            band = pl.ds(base, width)
            here = rows(block, BLOCK)
            both = qc[h, block]
            products = lax.dot_general(
                emb[band, :], both, (((1,), (1,)), ((), ())), preferred_element_type=F32
            )
            start = first[:, here] - base
            lane = lax.broadcasted_iota(jnp.int32, (BLOCK, BLOCK), 1) + (
                block * BLOCK - base
            )
            row = lax.broadcasted_iota(jnp.int32, (BLOCK, BLOCK), 0)
            scores = []
            for at in range(0, width, BLOCK):
                allowed = row + at >= start
                if at >= plain:
                    allowed = allowed & (row + at <= lane)
                scores.append(
                    jnp.where(allowed, products[at : at + BLOCK, :BLOCK], NEG)
                )
            highest = scores[0]
            for part in scores[1:]:
                highest = jnp.maximum(highest, part)
            highest = jnp.max(highest, axis=0, keepdims=True)
            total = jnp.zeros((BLOCK, BLOCK), F32)
            weighted = jnp.zeros((BLOCK, BLOCK), F32)
            weights = []
            for index, part in enumerate(scores):
                at = index * BLOCK
                value = jnp.exp2((part - highest) * log2_scaling)
                weights.append(value)
                total = total + value
                weighted = weighted + value * products[at : at + BLOCK, BLOCK:]
            share = 1.0 / jnp.sum(total, axis=0, keepdims=True)
            row_term = jnp.sum(weighted, axis=0, keepdims=True) * share
            scaled_share = share * scaling
            for index, value in enumerate(weights):
                at = index * BLOCK
                change = value * (products[at : at + BLOCK, BLOCK:] - row_term)
                pair[at : at + BLOCK, :BLOCK] = (change * scaled_share).astype(BF16)
                pair[at : at + BLOCK, BLOCK:] = (value * share).astype(BF16)
            dkv[band, :] += jnp.dot(
                pair[0:width, :], both, preferred_element_type=F32
            )
            queryT = jnp.dot(
                embT[:, band], pair[0:width, :BLOCK], preferred_element_type=F32
            )
            grad = queryT.T * gain_row + dkv[here, :]
            low = grad.astype(BF16).astype(F32)
            tile_here = of_tile(block)
            send_block[h, block] = jnp.where(tile_here, 0.0, low).astype(BF16)
            part = rows(lax.rem(block, tile_blocks), BLOCK)
            image[part, :] = jnp.where(
                tile_here, low, image[part, :].astype(F32)
            ).astype(BF16)

            target = out.at[
                0,
                :,
                pl.ds(pl.multiple_of(me * columns + h * HEAD, HEAD), HEAD),
            ]

            @pl.when(block == me)
            def _():
                pltpu.make_async_copy(
                    send_block.at[h, block], target, block_sem.at[h]
                ).start()

            @pl.when(block != me)
            def _():
                pltpu.make_async_remote_copy(
                    src_ref=send_block.at[h, block],
                    dst_ref=target,
                    send_sem=grad_send.at[h],
                    recv_sem=grad_recv.at[h],
                    device_id=seq_id(block),
                    device_id_type=MESH,
                ).start()

        reach = REACH // BLOCK

        def far(step, carry):
            block = n - 1 - step
            base = pl.multiple_of((block - reach) * BLOCK, BLOCK)
            attend(block, base, (reach + 1) * BLOCK, reach * BLOCK)
            return carry

        def near(high, low):
            def body(step, carry):
                attend(high - 1 - step, 0, high * BLOCK, low * BLOCK)
                return carry

            lax.fori_loop(0, high - low, body, 0)

        lax.fori_loop(0, n - reach, far, 0)
        near(reach, reach // 2)
        near(reach // 2, 0)

        tile_grad = image[...]

        def weight_rows(index, carry):
            mine = pl.multiple_of((2 * index + core) * out_rows, out_rows)
            theirs = pl.multiple_of((2 * index + 1 - core) * out_rows, out_rows)
            half_out[h, index] = jnp.dot(
                featT[pl.ds(theirs, out_rows), :],
                tile_grad,
                preferred_element_type=F32,
            ).astype(BF16)
            keep[index] = jnp.dot(
                featT[pl.ds(mine, out_rows), :],
                tile_grad,
                preferred_element_type=F32,
            )
            return carry

        lax.fori_loop(0, chips, weight_rows, 0)
        halves = pltpu.make_async_remote_copy(
            src_ref=half_out.at[h],
            dst_ref=half_in.at[h],
            send_sem=half_send.at[h],
            recv_sem=half_recv.at[h],
            device_id=(other_core, me),
            device_id_type=MESH,
        )
        halves.start()
        halves.wait()

        def add_halves(index, carry):
            value = keep[index] + half_in[h, index].astype(F32)
            keep[index] = value
            sum_out[h, index] = value.astype(BF16)
            return carry

        lax.fori_loop(0, chips, add_halves, 0)
        wgrad[:, head_cols] = keep[chip]

        def send_sums(d, carry):
            to = lax.rem(chip + d, chips)
            pltpu.make_async_remote_copy(
                src_ref=sum_out.at[h, to],
                dst_ref=sum_in.at[h, d - 1],
                send_sem=sum_send.at[h],
                recv_sem=sum_recv.at[h],
                device_id=(2 * to + core, me),
                device_id_type=MESH,
            ).start()
            return carry

        lax.fori_loop(1, chips, send_sums, 0)
        return head_carry

    lax.fori_loop(0, heads, one_head, 0)

    def finish(h, carry):
        head_cols = rows(h, HEAD)
        await_blocks(sum_in.at[h], sum_recv.at[h])
        total = wgrad[:, head_cols]
        for d in range(chips - 1):
            total = total + sum_in[h, d].astype(F32)
        wgrad[:, head_cols] = total * (1.0 / TILE_TOK)
        return carry

    lax.fori_loop(0, heads, finish, 0)

    for h in range(heads):
        sent = tx.at[h, pl.ds(0, peers * BLOCK)]
        await_blocks(sent, in_send.at[2 * h])
        await_blocks(sent, in_send.at[2 * h + 1])
        await_blocks(sum_in.at[h], sum_send.at[h])
        await_blocks(sent, grad_send.at[h])
        await_blocks(sent, grad_recv.at[h])
        pltpu.make_async_copy(
            send_block.at[h, 0], send_block.at[h, 0], block_sem.at[h]
        ).wait()
    for group in copies:
        for copy in group:
            copy.wait_send()


def per_device(
    n, enc, feat, weight, text, cot, gain, count, slot, doc
):
    heads = weight.shape[1] // HEAD
    depth = weight.shape[0]
    length = doc.shape[1]
    chips = enc // 2
    out_rows = depth // enc
    tile_rows = feat.shape[1] * n
    anywhere = pl.BlockSpec(memory_space=pl.ANY)
    vmem = pl.BlockSpec(memory_space=pltpu.VMEM)
    smem = pl.BlockSpec(memory_space=pltpu.SMEM)
    dma = pltpu.SemaphoreType.DMA
    ring_copies = 2 * (n // 4) + n // 2 + 2
    return pl.pallas_call(
        functools.partial(whole_kernel, n, heads, enc),
        out_shape=(
            jax.ShapeDtypeStruct(text.shape, BF16),
            jax.ShapeDtypeStruct((out_rows, heads * HEAD), F32),
        ),
        in_specs=[anywhere] * 4 + [vmem, smem, smem, vmem],
        out_specs=(anywhere, vmem),
        scratch_shapes=[
            pltpu.VMEM((tile_rows, depth), BF16),
            pltpu.VMEM((depth, tile_rows), BF16),
            pltpu.VMEM((depth, heads * HEAD), BF16),
            pltpu.VMEM((tile_rows, heads * HEAD), BF16),
            pltpu.VMEM((heads, length, HEAD), BF16),
            pltpu.VMEM((heads, n, 2 * BLOCK, HEAD), BF16),
            pltpu.VMEM((length, HEAD), BF16),
            pltpu.VMEM((HEAD, length), BF16),
            pltpu.VMEM((length, HEAD), F32),
            pltpu.VMEM((REACH + BLOCK, 2 * BLOCK), BF16),
            pltpu.VMEM((tile_rows, HEAD), BF16),
            pltpu.VMEM((heads, n, BLOCK, HEAD), BF16),
            pltpu.VMEM((1, length), jnp.int32),
            pltpu.VMEM((chips, out_rows, HEAD), F32),
            pltpu.VMEM((heads, chips, out_rows, HEAD), BF16),
            pltpu.VMEM((heads, chips, out_rows, HEAD), BF16),
            pltpu.VMEM((heads, chips, out_rows, HEAD), BF16),
            pltpu.VMEM((heads, chips - 1, out_rows, HEAD), BF16),
            dma((2 + 2 * heads,)),
            dma((ring_copies,)),
            dma((ring_copies,)),
            dma((2 * heads,)),
            dma((2 * heads,)),
            dma((heads,)),
            dma((heads,)),
            dma((heads,)),
            dma((heads,)),
            dma((heads,)),
            dma((heads,)),
            dma((heads,)),
        ],
        compiler_params=pltpu.CompilerParams(
            collective_id=0, has_side_effects=True, vmem_limit_bytes=48 * 2**20
        ),
    )(feat, weight, text, cot, gain.reshape(1, -1), count, slot, doc)


def solution(mesh):
    in_specs = (
        P("enc", "seq", None),
        P(None, "seq"),
        P("enc", "seq", None),
        P("enc", "seq", None),
        P("seq"),
        P("enc"),
        P("enc", None),
        P("enc", None),
    )
    out_specs = (P("enc", "seq", None), P("enc", "seq"))
    return jax.shard_map(
        functools.partial(per_device, mesh.shape["seq"], mesh.shape["enc"]),
        mesh=mesh,
        in_specs=in_specs,
        out_specs=out_specs,
        check_vma=False,
    )
```

```python
import functools

import jax
import jax.numpy as jnp
from jax import lax
from jax.experimental import pallas as pl
from jax.experimental.pallas import tpu as pltpu
from jax.sharding import PartitionSpec as P

HEAD = 128
TILE_TOK = 256
BLOCK = 128
GROUP = 256
REACH = 1024
DOC_VALUES = 8
NEG = -1e30
NT = (((1,), (1,)), ((), ()))
MESH = pl.DeviceIdType.MESH
F32 = jnp.float32
BF16 = jnp.bfloat16


def whole_kernel(
    n,
    heads,
    enc,
    feat,
    weight,
    text,
    cot,
    gain_in,
    count,
    slot,
    doc_in,
    out,
    wgrad,
    features,
    featT,
    wv,
    projected,
    tx,
    ct,
    queries,
    emb,
    embT,
    dkv,
    d_scores,
    probs,
    image,
    send_block,
    gain,
    doc,
    first,
    keep,
    half_out,
    half_in,
    sum_out,
    sum_in,
    local_sem,
    gather_send,
    gather_recv,
    in_send,
    in_recv,
    grad_send,
    grad_recv,
    half_send,
    half_recv,
    sum_send,
    sum_recv,
    block_sem,
):
    me = lax.axis_index("seq")
    my_enc = lax.axis_index("enc")
    core = lax.rem(my_enc, 2)
    chip = lax.div(my_enc, 2)
    chips = enc // 2
    other_core = my_enc + 1 - 2 * core
    beside = me + 1 - 2 * lax.rem(me, 2)
    columns = heads * HEAD
    shard = feat.shape[1]
    depth = feat.shape[2]
    length = n * BLOCK
    out_rows = depth // enc
    peers = n - 1

    def seq_id(index):
        return (my_enc, index)

    def along(step):
        return lax.rem(me + 2 * step + 2 * n, n)

    def rows(index, size):
        return pl.ds(pl.multiple_of(index * size, size), size)

    weight_copy = pltpu.make_async_copy(weight, wv, local_sem.at[0])
    weight_copy.start()
    own_features = pltpu.make_async_copy(
        feat.at[0], features.at[rows(me, shard)], local_sem.at[1]
    )
    own_features.start()
    own = []
    for h in range(heads):
        cols = pl.ds(pl.multiple_of(me * columns + h * HEAD, HEAD), HEAD)
        own.append(
            pltpu.make_async_copy(
                text.at[0, :, cols], tx.at[h, rows(me, BLOCK)], local_sem.at[2 + 2 * h]
            )
        )
        own.append(
            pltpu.make_async_copy(
                cot.at[0, :, cols],
                ct.at[h, rows(me, BLOCK)],
                local_sem.at[3 + 2 * h],
            )
        )
    for copy in own:
        copy.start()
    gain_copy = pltpu.make_async_copy(gain_in, gain, local_sem.at[2 + 2 * heads])
    gain_copy.start()
    doc_copy = pltpu.make_async_copy(doc_in, doc, local_sem.at[3 + 2 * heads])
    doc_copy.start()

    barrier = pltpu.get_barrier_semaphore()

    def greet_seq(d, carry):
        pl.semaphore_signal(
            barrier, inc=1, device_id=seq_id(lax.rem(me + d, n)), device_id_type=MESH
        )
        return carry

    def greet_enc(d, carry):
        to = 2 * lax.rem(chip + d, chips) + core
        pl.semaphore_signal(barrier, inc=1, device_id=(to, me), device_id_type=MESH)
        return carry

    lax.fori_loop(1, n, greet_seq, 0)
    lax.fori_loop(1, chips, greet_enc, 0)
    pl.semaphore_signal(barrier, inc=1, device_id=(other_core, me), device_id_type=MESH)
    pl.semaphore_wait(barrier, peers + chips)

    def pass_on(source, index, to, number, first_col=0, cols=depth):
        span = pl.ds(first_col, cols)
        place = features.at[rows(index, shard), span]
        return pltpu.make_async_remote_copy(
            src_ref=place if source is None else source,
            dst_ref=place,
            send_sem=gather_send.at[number],
            recv_sem=gather_recv.at[number],
            device_id=seq_id(to),
            device_id_type=MESH,
        )

    ring = n // 2
    ahead, behind = along(1), along(-1)
    full_steps = ring // 2 - 1
    half = depth // 2

    def exchange(h, source, to_cot, begin, end):
        def body(d, carry):
            to = lax.rem(me + d, n)
            cols = pl.ds(pl.multiple_of(to * columns + h * HEAD, HEAD), HEAD)
            place = (ct if to_cot else tx).at[h, rows(me, BLOCK)]
            pltpu.make_async_remote_copy(
                src_ref=source.at[0, :, cols],
                dst_ref=place,
                send_sem=in_send.at[2 * h + to_cot],
                recv_sem=in_recv.at[2 * h + to_cot],
                device_id=seq_id(to),
                device_id_type=MESH,
            ).start()
            return carry

        lax.fori_loop(begin, end, body, 0)

    def exchange_part(h, part, parts):
        begin = 1 + peers * part // parts
        end = 1 + peers * (part + 1) // parts
        exchange(h, text, 0, begin, end)
        exchange(h, cot, 1, begin, end)

    x_base = 2 * (full_steps + 1)
    copies = []
    parts = full_steps + 1
    for step in range(full_steps):
        if step == 0:
            source = feat.at[0]
            right = pass_on(source, me, ahead, 0)
            left = pass_on(source, me, behind, full_steps + 1)
            sideways = [pass_on(source, me, beside, x_base)]
        else:
            copies[-1][0].wait_recv()
            right = pass_on(None, along(-step), ahead, step)
            copies[-1][1].wait_recv()
            left = pass_on(None, along(step), behind, full_steps + 1 + step)
            sideways = [
                pass_on(None, along(-step), beside, x_base + 2 * step - 1),
                pass_on(None, along(step), beside, x_base + 2 * step),
            ]
        for copy in [right, left] + sideways:
            copy.start()
        copies.append([right, left] + sideways)
        exchange_part(0, step, parts)
    copies[-1][0].wait_recv()
    copies[-1][1].wait_recv()
    last = full_steps
    right = pass_on(None, along(-last), ahead, last, 0, half)
    left = pass_on(None, along(last), behind, full_steps + 1 + last, half, half)
    sideways = [
        pass_on(None, along(-last), beside, x_base + 2 * last - 1),
        pass_on(None, along(last), beside, x_base + 2 * last),
    ]
    for copy in [right, left] + sideways:
        copy.start()
    exchange_part(0, parts - 1, parts)
    right.wait_recv()
    left.wait_recv()
    farthest = pass_on(None, along(ring // 2), beside, x_base + 2 * last + 1)
    farthest.start()
    copies.append([right, left] + sideways + [farthest])

    for h in range(1, heads):
        exchange_part(h, 0, 1)

    doc_copy.wait()
    gain_copy.wait()
    doc_row = doc[...]
    begins = jnp.zeros_like(doc_row)
    for value in range(1, DOC_VALUES):
        below = jnp.sum((doc_row < value).astype(jnp.int32), axis=1, keepdims=True)
        begins = jnp.where(doc_row >= value, below, begins)
    first[...] = begins
    tile = jnp.where(count[0] > 0, slot[0, 0], -1)

    for group in copies:
        for copy in group[2:]:
            copy.wait_recv()
    own_features.wait()
    weight_copy.wait()

    projected[...] = jnp.dot(
        features[...], wv[...], preferred_element_type=F32
    ).astype(BF16)

    def turn_features(index, carry):
        place = rows(index, HEAD)
        featT[place, :] = features[:, place].T
        return carry

    lax.fori_loop(0, depth // HEAD, turn_features, 0)
    for copy in own:
        copy.wait()

    scaling = HEAD ** (-0.5)
    log2_scaling = scaling * 1.4426950408889634
    groups = length // GROUP
    group_reach = REACH // GROUP

    def await_blocks(like, sem):
        pltpu.make_async_copy(like, like, sem).wait()

    def prepare(h, gain_row):
        def body(index, carry):
            place = rows(index, GROUP)
            of_tile = jnp.full((GROUP, HEAD), tile, jnp.int32) == index
            value = jnp.where(
                of_tile,
                projected[:, h * HEAD : (h + 1) * HEAD].astype(F32),
                tx[h, place, :].astype(F32),
            )
            low = value.astype(BF16)
            emb[place, :] = low
            embT[:, place] = low.T
            queries[place, :] = (value * gain_row).astype(BF16)
            return carry

        lax.fori_loop(0, groups, body, 0)

    def score_part(h, index):
        least = max(0, index - group_reach)
        base, parts = least * GROUP, index + 1 - least
        here = pl.ds(index * GROUP, GROUP)
        query, cotangent = queries[here, :], ct[h, here, :]
        start = first[:, here] - base
        row = lax.broadcasted_iota(jnp.int32, (GROUP, GROUP), 0)
        lane = lax.broadcasted_iota(jnp.int32, (GROUP, GROUP), 1)
        scores, d_probs = [], []
        for part in range(parts):
            keys = emb[pl.ds(base + part * GROUP, GROUP), :]
            score = lax.dot_general(keys, query, NT, preferred_element_type=F32)
            d_probs.append(
                lax.dot_general(keys, cotangent, NT, preferred_element_type=F32)
            )
            allowed = row >= start - part * GROUP
            if part == parts - 1:
                allowed = allowed & (row <= lane)
            scores.append(jnp.where(allowed, score, NEG))
        highest = jnp.max(scores[0], axis=0, keepdims=True)
        for score in scores[1:]:
            highest = jnp.maximum(highest, jnp.max(score, axis=0, keepdims=True))
        total = jnp.zeros((1, GROUP), F32)
        weighted = jnp.zeros((1, GROUP), F32)
        weights = []
        for score, d_prob in zip(scores, d_probs):
            value = jnp.exp2((score - highest) * log2_scaling)
            weights.append(value)
            total = total + jnp.sum(value, axis=0, keepdims=True)
            weighted = weighted + jnp.sum(value * d_prob, axis=0, keepdims=True)
        share = 1.0 / total
        row_term = weighted * share
        scaled_share = share * scaling
        turn = index % 2
        for part, (value, d_prob) in enumerate(zip(weights, d_probs)):
            place = pl.ds(part * GROUP, GROUP)
            change = value * (d_prob - row_term)
            d_scores[turn, place, :] = (change * scaled_share).astype(BF16)
            probs[turn, place, :] = (value * share).astype(BF16)

    def product_part(h, index, gain_row):
        least = max(0, index - group_reach)
        width = (index + 1 - least) * GROUP
        band, here = pl.ds(least * GROUP, width), pl.ds(index * GROUP, GROUP)
        d_score = d_scores[index % 2, 0:width, :]
        dkv[band, :] += jnp.dot(
            d_score, queries[here, :], preferred_element_type=F32
        ) + jnp.dot(
            probs[index % 2, 0:width, :], ct[h, here, :], preferred_element_type=F32
        )
        queryT = jnp.dot(embT[:, band], d_score, preferred_element_type=F32)
        grad = queryT.T * gain_row + dkv[here, :]
        low = grad.astype(BF16).astype(F32)
        of_tile = jnp.full((GROUP, HEAD), tile, jnp.int32) == index
        send_block[h, here, :] = jnp.where(of_tile, 0.0, low).astype(BF16)
        image[...] = jnp.where(of_tile, low, image[...].astype(F32)).astype(BF16)

    def send_grad(h, block):
        source = send_block.at[h, rows(block, BLOCK)]
        target = out.at[
            0, :, pl.ds(pl.multiple_of(me * columns + h * HEAD, HEAD), HEAD)
        ]

        @pl.when(me == block)
        def _():
            pltpu.make_async_copy(source, target, block_sem.at[h]).start()

        @pl.when(me != block)
        def _():
            pltpu.make_async_remote_copy(
                src_ref=source,
                dst_ref=target,
                send_sem=grad_send.at[h],
                recv_sem=grad_recv.at[h],
                device_id=seq_id(block),
                device_id_type=MESH,
            ).start()

    def send_grads(h, begin, end):
        def body(step, carry):
            send_grad(h, end - 1 - step)
            return carry

        lax.fori_loop(0, end - begin, body, 0)

    def attend(h, gain_row, at_once):
        dkv[...] = jnp.zeros_like(dkv)
        image[...] = jnp.zeros_like(image)
        blocks = GROUP // BLOCK
        for index in range(groups - 1, -2, -1):
            if index >= 0:
                score_part(h, index)
            if index < groups - 1:
                product_part(h, index + 1, gain_row)
                if at_once:
                    send_grads(h, (index + 1) * blocks, (index + 2) * blocks)

    def weight_term(h):
        tile_grad = image[...]

        def weight_rows(index, carry):
            mine = pl.multiple_of((2 * index + core) * out_rows, out_rows)
            theirs = pl.multiple_of((2 * index + 1 - core) * out_rows, out_rows)
            half_out[h, index] = jnp.dot(
                featT[pl.ds(theirs, out_rows), :],
                tile_grad,
                preferred_element_type=F32,
            ).astype(BF16)
            keep[index] = jnp.dot(
                featT[pl.ds(mine, out_rows), :],
                tile_grad,
                preferred_element_type=F32,
            )
            return carry

        lax.fori_loop(0, chips, weight_rows, 0)
        halves = pltpu.make_async_remote_copy(
            src_ref=half_out.at[h],
            dst_ref=half_in.at[h],
            send_sem=half_send.at[h],
            recv_sem=half_recv.at[h],
            device_id=(other_core, me),
            device_id_type=MESH,
        )
        halves.start()
        return halves

    def send_sums(h, halves):
        halves.wait()

        def add_halves(index, carry):
            value = keep[index] + half_in[h, index].astype(F32)
            keep[index] = value
            sum_out[h, index] = value.astype(BF16)
            return carry

        lax.fori_loop(0, chips, add_halves, 0)
        wgrad[:, h * HEAD : (h + 1) * HEAD] = keep[chip]

        def body(d, carry):
            to = lax.rem(chip + d, chips)
            pltpu.make_async_remote_copy(
                src_ref=sum_out.at[h, to],
                dst_ref=sum_in.at[h, d - 1],
                send_sem=sum_send.at[h],
                recv_sem=sum_recv.at[h],
                device_id=(2 * to + core, me),
                device_id_type=MESH,
            ).start()
            return carry

        lax.fori_loop(1, chips, body, 0)

    def finish(h):
        cols = slice(h * HEAD, (h + 1) * HEAD)
        await_blocks(sum_in.at[h], sum_recv.at[h])
        total = wgrad[:, cols]
        for d in range(chips - 1):
            total = total + sum_in[h, d].astype(F32)
        wgrad[:, cols] = total * (1.0 / TILE_TOK)

    for h in range(heads):
        gain_row = gain[:, h * HEAD : (h + 1) * HEAD]
        arrived = tx.at[h, pl.ds(0, peers * BLOCK)]
        await_blocks(arrived, in_recv.at[2 * h])
        prepare(h, gain_row)
        await_blocks(arrived, in_recv.at[2 * h + 1])
        if h > 0:
            send_grads(h - 1, 0, n)
        attend(h, gain_row, h == heads - 1)
        halves = weight_term(h)
        if h > 0:
            finish(h - 1)
        send_sums(h, halves)
    finish(heads - 1)

    for h in range(heads):
        sent = tx.at[h, pl.ds(0, peers * BLOCK)]
        await_blocks(sent, in_send.at[2 * h])
        await_blocks(sent, in_send.at[2 * h + 1])
        await_blocks(sum_in.at[h], sum_send.at[h])
        await_blocks(sent, grad_send.at[h])
        await_blocks(sent, grad_recv.at[h])
        own_block = send_block.at[h, pl.ds(0, BLOCK)]
        await_blocks(own_block, block_sem.at[h])
    for group in copies:
        for copy in group:
            copy.wait_send()


def per_device(
    n, enc, feat, weight, text, cot, gain, count, slot, doc
):
    heads = weight.shape[1] // HEAD
    depth = weight.shape[0]
    length = doc.shape[1]
    chips = enc // 2
    out_rows = depth // enc
    tile_rows = feat.shape[1] * n
    anywhere = pl.BlockSpec(memory_space=pl.ANY)
    hbm = pl.BlockSpec(memory_space=pltpu.HBM)
    vmem = pl.BlockSpec(memory_space=pltpu.VMEM)
    smem = pl.BlockSpec(memory_space=pltpu.SMEM)
    dma = pltpu.SemaphoreType.DMA
    ring_copies = 2 * (n // 4) + n // 2 + 2
    return pl.pallas_call(
        functools.partial(whole_kernel, n, heads, enc),
        out_shape=(
            jax.ShapeDtypeStruct(text.shape, BF16),
            jax.ShapeDtypeStruct((out_rows, heads * HEAD), F32),
        ),
        in_specs=[hbm] * 5 + [smem, smem, hbm],
        out_specs=(anywhere, vmem),
        scratch_shapes=[
            pltpu.VMEM((tile_rows, depth), BF16),
            pltpu.VMEM((depth, tile_rows), BF16),
            pltpu.VMEM((depth, heads * HEAD), BF16),
            pltpu.VMEM((tile_rows, heads * HEAD), BF16),
            pltpu.VMEM((heads, length, HEAD), BF16),
            pltpu.VMEM((heads, length, HEAD), BF16),
            pltpu.VMEM((length, HEAD), BF16),
            pltpu.VMEM((length, HEAD), BF16),
            pltpu.VMEM((HEAD, length), BF16),
            pltpu.VMEM((length, HEAD), F32),
            pltpu.VMEM((2, REACH + GROUP, GROUP), BF16),
            pltpu.VMEM((2, REACH + GROUP, GROUP), BF16),
            pltpu.VMEM((tile_rows, HEAD), BF16),
            pltpu.VMEM((heads, length, HEAD), BF16),
            pltpu.VMEM((1, heads * HEAD), F32),
            pltpu.VMEM((1, length), jnp.int32),
            pltpu.VMEM((1, length), jnp.int32),
            pltpu.VMEM((chips, out_rows, HEAD), F32),
            pltpu.VMEM((heads, chips, out_rows, HEAD), BF16),
            pltpu.VMEM((heads, chips, out_rows, HEAD), BF16),
            pltpu.VMEM((heads, chips, out_rows, HEAD), BF16),
            pltpu.VMEM((heads, chips - 1, out_rows, HEAD), BF16),
            dma((4 + 2 * heads,)),
            dma((ring_copies,)),
            dma((ring_copies,)),
            dma((2 * heads,)),
            dma((2 * heads,)),
            dma((heads,)),
            dma((heads,)),
            dma((heads,)),
            dma((heads,)),
            dma((heads,)),
            dma((heads,)),
            dma((heads,)),
        ],
        compiler_params=pltpu.CompilerParams(
            collective_id=0, has_side_effects=True, vmem_limit_bytes=60 * 2**20
        ),
    )(feat, weight, text, cot, gain.reshape(1, -1), count, slot, doc)


def solution(mesh):
    in_specs = (
        P("enc", "seq", None),
        P(None, "seq"),
        P("enc", "seq", None),
        P("enc", "seq", None),
        P("seq"),
        P("enc"),
        P("enc", None),
        P("enc", None),
    )
    out_specs = (P("enc", "seq", None), P("enc", "seq"))
    return jax.shard_map(
        functools.partial(per_device, mesh.shape["seq"], mesh.shape["enc"]),
        mesh=mesh,
        in_specs=in_specs,
        out_specs=out_specs,
        check_vma=False,
    )
```

```python
import functools

import jax
import jax.numpy as jnp
from jax import lax
from jax.experimental import pallas as pl
from jax.experimental.pallas import tpu as pltpu
from jax.sharding import PartitionSpec as P

HEAD = 128
TILE_TOK = 256
BLOCK = 128
GROUP = 256
REACH = 1024
DOC_VALUES = 8
NEG = -1e30
NT = (((1,), (1,)), ((), ()))
MESH = pl.DeviceIdType.MESH
F32 = jnp.float32
BF16 = jnp.bfloat16


def whole_kernel(
    n,
    heads,
    enc,
    feat,
    weight,
    text,
    cot,
    gain_in,
    count,
    slot,
    doc_in,
    out,
    wgrad,
    features,
    featT,
    wv,
    projected,
    tx,
    ct,
    queries,
    emb,
    embT,
    dkv,
    d_scores,
    probs,
    image,
    send_block,
    gain,
    doc,
    first,
    keep,
    half_out,
    half_in,
    sum_out,
    sum_in,
    local_sem,
    gather_send,
    gather_recv,
    in_send,
    in_recv,
    grad_send,
    grad_recv,
    half_send,
    half_recv,
    sum_send,
    sum_recv,
    block_sem,
):
    me = lax.axis_index("seq")
    my_enc = lax.axis_index("enc")
    core = lax.rem(my_enc, 2)
    chip = lax.div(my_enc, 2)
    chips = enc // 2
    other_core = my_enc + 1 - 2 * core
    beside = me + 1 - 2 * lax.rem(me, 2)
    columns = heads * HEAD
    shard = feat.shape[1]
    depth = feat.shape[2]
    length = n * BLOCK
    out_rows = depth // enc
    peers = n - 1

    def seq_id(index):
        return (my_enc, index)

    def along(step):
        return lax.rem(me + 2 * step + 2 * n, n)

    def partner(step):
        away = n // 2 - lax.div(step + 1, 2)
        return lax.rem(me + n + away * (1 - 2 * lax.rem(step, 2)), n)

    def rows(index, size):
        return pl.ds(pl.multiple_of(index * size, size), size)

    barrier = pltpu.get_barrier_semaphore()

    def greet_seq(d, carry):
        pl.semaphore_signal(
            barrier, inc=1, device_id=seq_id(lax.rem(me + d, n)), device_id_type=MESH
        )
        return carry

    def greet_enc(d, carry):
        to = 2 * lax.rem(chip + d, chips) + core
        pl.semaphore_signal(barrier, inc=1, device_id=(to, me), device_id_type=MESH)
        return carry

    lax.fori_loop(1, n, greet_seq, 0)
    lax.fori_loop(1, chips, greet_enc, 0)
    pl.semaphore_signal(barrier, inc=1, device_id=(other_core, me), device_id_type=MESH)

    weight_copy = pltpu.make_async_copy(weight, wv, local_sem.at[0])
    weight_copy.start()
    own_features = pltpu.make_async_copy(
        feat.at[0], features.at[rows(me, shard)], local_sem.at[1]
    )
    own_features.start()
    own = []
    for h in range(heads):
        cols = pl.ds(pl.multiple_of(me * columns + h * HEAD, HEAD), HEAD)
        own.append(
            pltpu.make_async_copy(
                text.at[0, :, cols], tx.at[h, rows(me, BLOCK)], local_sem.at[2 + 2 * h]
            )
        )
        own.append(
            pltpu.make_async_copy(
                cot.at[0, :, cols],
                ct.at[h, rows(me, BLOCK)],
                local_sem.at[3 + 2 * h],
            )
        )
    for copy in own:
        copy.start()
    gain_copy = pltpu.make_async_copy(gain_in, gain, local_sem.at[2 + 2 * heads])
    gain_copy.start()
    doc_copy = pltpu.make_async_copy(doc_in, doc, local_sem.at[3 + 2 * heads])
    doc_copy.start()

    pl.semaphore_wait(barrier, peers + chips)

    def pass_on(source, index, to, number, first_col=0, cols=depth):
        span = pl.ds(first_col, cols)
        place = features.at[rows(index, shard), span]
        return pltpu.make_async_remote_copy(
            src_ref=place if source is None else source,
            dst_ref=place,
            send_sem=gather_send.at[number],
            recv_sem=gather_recv.at[number],
            device_id=seq_id(to),
            device_id_type=MESH,
        )

    ring = n // 2
    ahead, behind = along(1), along(-1)
    full_steps = ring // 2 - 1
    half = depth // 2

    def exchange(h, source, to_cot, begin, end):
        def body(step, carry):
            to = partner(step)
            cols = pl.ds(pl.multiple_of(to * columns + h * HEAD, HEAD), HEAD)
            place = (ct if to_cot else tx).at[h, rows(me, BLOCK)]
            pltpu.make_async_remote_copy(
                src_ref=source.at[0, :, cols],
                dst_ref=place,
                send_sem=in_send.at[2 * h + to_cot],
                recv_sem=in_recv.at[2 * h + to_cot],
                device_id=seq_id(to),
                device_id_type=MESH,
            ).start()
            return carry

        lax.fori_loop(begin, end, body, 0)

    def exchange_part(h, part, parts):
        begin = peers * part // parts
        end = peers * (part + 1) // parts
        exchange(h, text, 0, begin, end)
        exchange(h, cot, 1, begin, end)

    x_base = 2 * (full_steps + 1)
    copies = []
    parts = full_steps + 1
    for step in range(full_steps):
        if step == 0:
            source = feat.at[0]
            right = pass_on(source, me, ahead, 0)
            left = pass_on(source, me, behind, full_steps + 1)
            sideways = [pass_on(source, me, beside, x_base)]
        else:
            copies[-1][0].wait_recv()
            right = pass_on(None, along(-step), ahead, step)
            copies[-1][1].wait_recv()
            left = pass_on(None, along(step), behind, full_steps + 1 + step)
            sideways = [
                pass_on(None, along(-step), beside, x_base + 2 * step - 1),
                pass_on(None, along(step), beside, x_base + 2 * step),
            ]
        for copy in [right, left] + sideways:
            copy.start()
        copies.append([right, left] + sideways)
        exchange_part(0, step, parts)
    copies[-1][0].wait_recv()
    copies[-1][1].wait_recv()
    last = full_steps
    right = pass_on(None, along(-last), ahead, last, 0, half)
    left = pass_on(None, along(last), behind, full_steps + 1 + last, half, half)
    sideways = [
        pass_on(None, along(-last), beside, x_base + 2 * last - 1),
        pass_on(None, along(last), beside, x_base + 2 * last),
    ]
    for copy in [right, left] + sideways:
        copy.start()
    exchange_part(0, parts - 1, parts)
    right.wait_recv()
    left.wait_recv()
    farthest = pass_on(None, along(ring // 2), beside, x_base + 2 * last + 1)
    farthest.start()
    copies.append([right, left] + sideways + [farthest])

    for h in range(1, heads):
        exchange_part(h, 0, 1)

    doc_copy.wait()
    gain_copy.wait()
    doc_row = doc[...]
    begins = jnp.zeros_like(doc_row)
    for value in range(1, DOC_VALUES):
        below = jnp.sum((doc_row < value).astype(jnp.int32), axis=1, keepdims=True)
        begins = jnp.where(doc_row >= value, below, begins)
    first[...] = begins
    tile = jnp.where(count[0] > 0, slot[0, 0], -1)

    for group in copies:
        for copy in group[2:]:
            copy.wait_recv()
    own_features.wait()
    weight_copy.wait()

    projected[...] = jnp.dot(
        features[...], wv[...], preferred_element_type=F32
    ).astype(BF16)

    def turn_features(index, carry):
        place = rows(index, HEAD)
        featT[place, :] = features[:, place].T
        return carry

    lax.fori_loop(0, depth // HEAD, turn_features, 0)
    for copy in own:
        copy.wait()

    scaling = HEAD ** (-0.5)
    log2_scaling = scaling * 1.4426950408889634
    groups = length // GROUP
    group_reach = REACH // GROUP

    def await_blocks(like, sem):
        pltpu.make_async_copy(like, like, sem).wait()

    def prepare(h, gain_row):
        def body(index, carry):
            place = rows(index, GROUP)
            of_tile = jnp.full((GROUP, HEAD), tile, jnp.int32) == index
            value = jnp.where(
                of_tile,
                projected[:, h * HEAD : (h + 1) * HEAD].astype(F32),
                tx[h, place, :].astype(F32),
            )
            low = value.astype(BF16)
            emb[place, :] = low
            embT[:, place] = low.T
            queries[place, :] = (value * gain_row).astype(BF16)
            return carry

        lax.fori_loop(0, groups, body, 0)

    def score_part(h, index):
        least = max(0, index - group_reach)
        base, parts = least * GROUP, index + 1 - least
        here = pl.ds(index * GROUP, GROUP)
        query, cotangent = queries[here, :], ct[h, here, :]
        start = first[:, here] - base
        row = lax.broadcasted_iota(jnp.int32, (GROUP, GROUP), 0)
        lane = lax.broadcasted_iota(jnp.int32, (GROUP, GROUP), 1)
        scores, d_probs = [], []
        for part in range(parts):
            keys = emb[pl.ds(base + part * GROUP, GROUP), :]
            score = lax.dot_general(keys, query, NT, preferred_element_type=F32)
            d_probs.append(
                lax.dot_general(keys, cotangent, NT, preferred_element_type=F32)
            )
            allowed = row >= start - part * GROUP
            if part == parts - 1:
                allowed = allowed & (row <= lane)
            scores.append(jnp.where(allowed, score, NEG))
        highest = jnp.max(scores[0], axis=0, keepdims=True)
        for score in scores[1:]:
            highest = jnp.maximum(highest, jnp.max(score, axis=0, keepdims=True))
        total = jnp.zeros((1, GROUP), F32)
        weighted = jnp.zeros((1, GROUP), F32)
        weights = []
        for score, d_prob in zip(scores, d_probs):
            value = jnp.exp2((score - highest) * log2_scaling)
            weights.append(value)
            total = total + jnp.sum(value, axis=0, keepdims=True)
            weighted = weighted + jnp.sum(value * d_prob, axis=0, keepdims=True)
        share = 1.0 / total
        row_term = weighted * share
        scaled_share = share * scaling
        turn = index % 2
        for part, (value, d_prob) in enumerate(zip(weights, d_probs)):
            place = pl.ds(part * GROUP, GROUP)
            change = value * (d_prob - row_term)
            d_scores[turn, place, :] = (change * scaled_share).astype(BF16)
            probs[turn, place, :] = (value * share).astype(BF16)

    def product_part(h, index, gain_row):
        least = max(0, index - group_reach)
        width = (index + 1 - least) * GROUP
        band, here = pl.ds(least * GROUP, width), pl.ds(index * GROUP, GROUP)
        d_score = d_scores[index % 2, 0:width, :]
        dkv[band, :] += jnp.dot(
            d_score, queries[here, :], preferred_element_type=F32
        ) + jnp.dot(
            probs[index % 2, 0:width, :], ct[h, here, :], preferred_element_type=F32
        )
        queryT = jnp.dot(embT[:, band], d_score, preferred_element_type=F32)
        grad = queryT.T * gain_row + dkv[here, :]
        low = grad.astype(BF16).astype(F32)
        of_tile = jnp.full((GROUP, HEAD), tile, jnp.int32) == index
        send_block[h, here, :] = jnp.where(of_tile, 0.0, low).astype(BF16)
        image[...] = jnp.where(of_tile, low, image[...].astype(F32)).astype(BF16)

    def send_grads(h, least, most):
        target = out.at[
            0, :, pl.ds(pl.multiple_of(me * columns + h * HEAD, HEAD), HEAD)
        ]

        def body(step, carry):
            to = partner(step)

            @pl.when((to >= least) & (to < most))
            def _():
                pltpu.make_async_remote_copy(
                    src_ref=send_block.at[h, rows(to, BLOCK)],
                    dst_ref=target,
                    send_sem=grad_send.at[h],
                    recv_sem=grad_recv.at[h],
                    device_id=seq_id(to),
                    device_id_type=MESH,
                ).start()

            return carry

        lax.fori_loop(0, peers, body, 0)

        @pl.when((me >= least) & (me < most))
        def _():
            pltpu.make_async_copy(
                send_block.at[h, rows(me, BLOCK)], target, block_sem.at[h]
            ).start()

    def attend(h, gain_row):
        dkv[...] = jnp.zeros_like(dkv)
        image[...] = jnp.zeros_like(image)
        for index in range(groups - 1, -2, -1):
            if index >= 0:
                score_part(h, index)
            if index < groups - 1:
                product_part(h, index + 1, gain_row)
            if index in (groups // 2 - 1, -1):
                done = (index + 1) * GROUP // BLOCK
                if h == heads - 1:
                    send_grads(h, done, done + n // 2)

    def weight_term(h):
        tile_grad = image[...]

        def weight_rows(index, carry):
            mine = pl.multiple_of((2 * index + core) * out_rows, out_rows)
            theirs = pl.multiple_of((2 * index + 1 - core) * out_rows, out_rows)
            half_out[h, index] = jnp.dot(
                featT[pl.ds(theirs, out_rows), :],
                tile_grad,
                preferred_element_type=F32,
            ).astype(BF16)
            keep[index] = jnp.dot(
                featT[pl.ds(mine, out_rows), :],
                tile_grad,
                preferred_element_type=F32,
            )
            return carry

        lax.fori_loop(0, chips, weight_rows, 0)
        halves = pltpu.make_async_remote_copy(
            src_ref=half_out.at[h],
            dst_ref=half_in.at[h],
            send_sem=half_send.at[h],
            recv_sem=half_recv.at[h],
            device_id=(other_core, me),
            device_id_type=MESH,
        )
        halves.start()
        return halves

    def send_sums(h, halves):
        halves.wait()

        def add_halves(index, carry):
            value = keep[index] + half_in[h, index].astype(F32)
            keep[index] = value
            sum_out[h, index] = value.astype(BF16)
            return carry

        lax.fori_loop(0, chips, add_halves, 0)
        wgrad[:, h * HEAD : (h + 1) * HEAD] = keep[chip]

        def body(d, carry):
            to = lax.rem(chip + d, chips)
            pltpu.make_async_remote_copy(
                src_ref=sum_out.at[h, to],
                dst_ref=sum_in.at[h, d - 1],
                send_sem=sum_send.at[h],
                recv_sem=sum_recv.at[h],
                device_id=(2 * to + core, me),
                device_id_type=MESH,
            ).start()
            return carry

        lax.fori_loop(1, chips, body, 0)

    def finish(h):
        cols = slice(h * HEAD, (h + 1) * HEAD)
        await_blocks(sum_in.at[h], sum_recv.at[h])
        total = wgrad[:, cols]
        for d in range(chips - 1):
            total = total + sum_in[h, d].astype(F32)
        wgrad[:, cols] = total * (1.0 / TILE_TOK)

    for h in range(heads):
        gain_row = gain[:, h * HEAD : (h + 1) * HEAD]
        arrived = tx.at[h, pl.ds(0, peers * BLOCK)]
        await_blocks(arrived, in_recv.at[2 * h])
        prepare(h, gain_row)
        await_blocks(arrived, in_recv.at[2 * h + 1])
        if h > 0:
            send_grads(h - 1, 0, n)
        attend(h, gain_row)
        halves = weight_term(h)
        if h > 0:
            finish(h - 1)
        send_sums(h, halves)
    finish(heads - 1)

    for h in range(heads):
        sent = tx.at[h, pl.ds(0, peers * BLOCK)]
        await_blocks(sent, in_send.at[2 * h])
        await_blocks(sent, in_send.at[2 * h + 1])
        await_blocks(sum_in.at[h], sum_send.at[h])
        await_blocks(sent, grad_send.at[h])
        await_blocks(sent, grad_recv.at[h])
        own_block = send_block.at[h, pl.ds(0, BLOCK)]
        await_blocks(own_block, block_sem.at[h])
    for group in copies:
        for copy in group:
            copy.wait_send()


def per_device(
    n, enc, feat, weight, text, cot, gain, count, slot, doc
):
    heads = weight.shape[1] // HEAD
    depth = weight.shape[0]
    length = doc.shape[1]
    chips = enc // 2
    out_rows = depth // enc
    tile_rows = feat.shape[1] * n
    anywhere = pl.BlockSpec(memory_space=pl.ANY)
    hbm = pl.BlockSpec(memory_space=pltpu.HBM)
    vmem = pl.BlockSpec(memory_space=pltpu.VMEM)
    smem = pl.BlockSpec(memory_space=pltpu.SMEM)
    dma = pltpu.SemaphoreType.DMA
    ring_copies = 2 * (n // 4) + n // 2 + 2
    return pl.pallas_call(
        functools.partial(whole_kernel, n, heads, enc),
        out_shape=(
            jax.ShapeDtypeStruct(text.shape, BF16),
            jax.ShapeDtypeStruct((out_rows, heads * HEAD), F32),
        ),
        in_specs=[hbm] * 5 + [smem, smem, hbm],
        out_specs=(anywhere, vmem),
        scratch_shapes=[
            pltpu.VMEM((tile_rows, depth), BF16),
            pltpu.VMEM((depth, tile_rows), BF16),
            pltpu.VMEM((depth, heads * HEAD), BF16),
            pltpu.VMEM((tile_rows, heads * HEAD), BF16),
            pltpu.VMEM((heads, length, HEAD), BF16),
            pltpu.VMEM((heads, length, HEAD), BF16),
            pltpu.VMEM((length, HEAD), BF16),
            pltpu.VMEM((length, HEAD), BF16),
            pltpu.VMEM((HEAD, length), BF16),
            pltpu.VMEM((length, HEAD), F32),
            pltpu.VMEM((2, REACH + GROUP, GROUP), BF16),
            pltpu.VMEM((2, REACH + GROUP, GROUP), BF16),
            pltpu.VMEM((tile_rows, HEAD), BF16),
            pltpu.VMEM((heads, length, HEAD), BF16),
            pltpu.VMEM((1, heads * HEAD), F32),
            pltpu.VMEM((1, length), jnp.int32),
            pltpu.VMEM((1, length), jnp.int32),
            pltpu.VMEM((chips, out_rows, HEAD), F32),
            pltpu.VMEM((heads, chips, out_rows, HEAD), BF16),
            pltpu.VMEM((heads, chips, out_rows, HEAD), BF16),
            pltpu.VMEM((heads, chips, out_rows, HEAD), BF16),
            pltpu.VMEM((heads, chips - 1, out_rows, HEAD), BF16),
            dma((4 + 2 * heads,)),
            dma((ring_copies,)),
            dma((ring_copies,)),
            dma((2 * heads,)),
            dma((2 * heads,)),
            dma((heads,)),
            dma((heads,)),
            dma((heads,)),
            dma((heads,)),
            dma((heads,)),
            dma((heads,)),
            dma((heads,)),
        ],
        compiler_params=pltpu.CompilerParams(
            collective_id=0, has_side_effects=True, vmem_limit_bytes=60 * 2**20
        ),
    )(feat, weight, text, cot, gain.reshape(1, -1), count, slot, doc)


def solution(mesh):
    in_specs = (
        P("enc", "seq", None),
        P(None, "seq"),
        P("enc", "seq", None),
        P("enc", "seq", None),
        P("seq"),
        P("enc"),
        P("enc", None),
        P("enc", None),
    )
    out_specs = (P("enc", "seq", None), P("enc", "seq"))
    return jax.shard_map(
        functools.partial(per_device, mesh.shape["seq"], mesh.shape["enc"]),
        mesh=mesh,
        in_specs=in_specs,
        out_specs=out_specs,
        check_vma=False,
    )
```

```python
import functools

import jax
import jax.numpy as jnp
from jax import lax
from jax.experimental import pallas as pl
from jax.experimental.pallas import tpu as pltpu
from jax.sharding import PartitionSpec as P

HEAD = 128
TILE_TOK = 256
BLOCK = 128
GROUP = 256
REACH = 1024
DOC_VALUES = 8
NEG = -1e30
NT = (((1,), (1,)), ((), ()))
MESH = pl.DeviceIdType.MESH
F32 = jnp.float32
BF16 = jnp.bfloat16


def whole_kernel(
    n,
    heads,
    enc,
    feat,
    weight,
    text,
    cot,
    gain_in,
    count,
    slot,
    doc_in,
    out,
    wgrad,
    features,
    featT,
    wv,
    projected,
    tx,
    ct,
    queries,
    emb,
    embT,
    dkv,
    d_scores,
    probs,
    image,
    send_block,
    gain,
    doc,
    first,
    keep,
    half_out,
    half_in,
    sum_out,
    sum_in,
    local_sem,
    gather_send,
    gather_recv,
    in_send,
    in_recv,
    grad_send,
    grad_recv,
    half_send,
    half_recv,
    sum_send,
    sum_recv,
    block_sem,
):
    me = lax.axis_index("seq")
    my_enc = lax.axis_index("enc")
    core = lax.rem(my_enc, 2)
    chip = lax.div(my_enc, 2)
    chips = enc // 2
    other_core = my_enc + 1 - 2 * core
    beside = me + 1 - 2 * lax.rem(me, 2)
    columns = heads * HEAD
    shard = feat.shape[1]
    depth = feat.shape[2]
    length = n * BLOCK
    out_rows = depth // enc
    peers = n - 1

    def seq_id(index):
        return (my_enc, index)

    def along(step):
        return lax.rem(me + 2 * step + 2 * n, n)

    def partner(step):
        away = n // 2 - lax.div(step + 1, 2)
        return lax.rem(me + n + away * (1 - 2 * lax.rem(step, 2)), n)

    def rows(index, size):
        return pl.ds(pl.multiple_of(index * size, size), size)

    barrier = pltpu.get_barrier_semaphore()

    def greet_seq(d, carry):
        pl.semaphore_signal(
            barrier, inc=1, device_id=seq_id(lax.rem(me + d, n)), device_id_type=MESH
        )
        return carry

    def greet_enc(d, carry):
        to = 2 * lax.rem(chip + d, chips) + core
        pl.semaphore_signal(barrier, inc=1, device_id=(to, me), device_id_type=MESH)
        return carry

    lax.fori_loop(1, n, greet_seq, 0)
    lax.fori_loop(1, chips, greet_enc, 0)
    pl.semaphore_signal(barrier, inc=1, device_id=(other_core, me), device_id_type=MESH)

    weight_copy = pltpu.make_async_copy(weight, wv, local_sem.at[0])
    weight_copy.start()
    own_features = pltpu.make_async_copy(
        feat.at[0], features.at[rows(me, shard)], local_sem.at[1]
    )
    own_features.start()
    own = []
    for h in range(heads):
        cols = pl.ds(pl.multiple_of(me * columns + h * HEAD, HEAD), HEAD)
        own.append(
            pltpu.make_async_copy(
                text.at[0, :, cols], tx.at[h, rows(me, BLOCK)], local_sem.at[2 + 2 * h]
            )
        )
        own.append(
            pltpu.make_async_copy(
                cot.at[0, :, cols],
                ct.at[h, rows(me, BLOCK)],
                local_sem.at[3 + 2 * h],
            )
        )
    for copy in own:
        copy.start()
    gain_copy = pltpu.make_async_copy(gain_in, gain, local_sem.at[2 + 2 * heads])
    gain_copy.start()
    doc_copy = pltpu.make_async_copy(doc_in, doc, local_sem.at[3 + 2 * heads])
    doc_copy.start()

    pl.semaphore_wait(barrier, peers + chips)

    def pass_on(source, index, to, number, first_col=0, cols=depth):
        span = pl.ds(first_col, cols)
        place = features.at[rows(index, shard), span]
        return pltpu.make_async_remote_copy(
            src_ref=place if source is None else source,
            dst_ref=place,
            send_sem=gather_send.at[number],
            recv_sem=gather_recv.at[number],
            device_id=seq_id(to),
            device_id_type=MESH,
        )

    ring = n // 2
    ahead, behind = along(1), along(-1)
    full_steps = ring // 2 - 1
    half = depth // 2

    def exchange(h, source, to_cot, begin, end):
        def body(step, carry):
            to = partner(step)
            cols = pl.ds(pl.multiple_of(to * columns + h * HEAD, HEAD), HEAD)
            place = (ct if to_cot else tx).at[h, rows(me, BLOCK)]
            pltpu.make_async_remote_copy(
                src_ref=source.at[0, :, cols],
                dst_ref=place,
                send_sem=in_send.at[2 * h + to_cot],
                recv_sem=in_recv.at[2 * h + to_cot],
                device_id=seq_id(to),
                device_id_type=MESH,
            ).start()
            return carry

        lax.fori_loop(begin, end, body, 0)

    def exchange_part(h, part, parts):
        begin = peers * part // parts
        end = peers * (part + 1) // parts
        exchange(h, text, 0, begin, end)
        exchange(h, cot, 1, begin, end)

    x_base = 2 * (full_steps + 1)
    copies = []
    parts = full_steps + 1
    for step in range(full_steps):
        if step == 0:
            source = feat.at[0]
            right = pass_on(source, me, ahead, 0)
            left = pass_on(source, me, behind, full_steps + 1)
            sideways = [pass_on(source, me, beside, x_base)]
        else:
            copies[-1][0].wait_recv()
            right = pass_on(None, along(-step), ahead, step)
            copies[-1][1].wait_recv()
            left = pass_on(None, along(step), behind, full_steps + 1 + step)
            sideways = [
                pass_on(None, along(-step), beside, x_base + 2 * step - 1),
                pass_on(None, along(step), beside, x_base + 2 * step),
            ]
        for copy in [right, left] + sideways:
            copy.start()
        copies.append([right, left] + sideways)
        exchange_part(0, step, parts)
    copies[-1][0].wait_recv()
    copies[-1][1].wait_recv()
    last = full_steps
    right = pass_on(None, along(-last), ahead, last, 0, half)
    left = pass_on(None, along(last), behind, full_steps + 1 + last, half, half)
    sideways = [
        pass_on(None, along(-last), beside, x_base + 2 * last - 1),
        pass_on(None, along(last), beside, x_base + 2 * last),
    ]
    for copy in [right, left] + sideways:
        copy.start()
    exchange_part(0, parts - 1, parts)
    right.wait_recv()
    left.wait_recv()
    farthest = pass_on(None, along(ring // 2), beside, x_base + 2 * last + 1)
    farthest.start()
    copies.append([right, left] + sideways + [farthest])

    for h in range(1, heads):
        exchange_part(h, 0, 1)

    doc_copy.wait()
    gain_copy.wait()
    doc_row = doc[...]
    begins = jnp.zeros_like(doc_row)
    for value in range(1, DOC_VALUES):
        below = jnp.sum((doc_row < value).astype(jnp.int32), axis=1, keepdims=True)
        begins = jnp.where(doc_row >= value, below, begins)
    first[...] = begins
    tile = jnp.where(count[0] > 0, slot[0, 0], -1)

    for group in copies:
        for copy in group[2:]:
            copy.wait_recv()
    own_features.wait()
    weight_copy.wait()

    projected[...] = jnp.dot(
        features[...], wv[...], preferred_element_type=F32
    ).astype(BF16)

    def turn_features(index, carry):
        place = rows(index, HEAD)
        featT[place, :] = features[:, place].T
        return carry

    lax.fori_loop(0, depth // HEAD, turn_features, 0)
    for copy in own:
        copy.wait()

    scaling = HEAD ** (-0.5)
    log2_scaling = scaling * 1.4426950408889634
    groups = length // GROUP
    group_reach = REACH // GROUP

    def await_blocks(like, sem):
        pltpu.make_async_copy(like, like, sem).wait()

    def prepare(h, gain_row):
        def body(index, carry):
            place = rows(index, GROUP)
            of_tile = jnp.full((GROUP, HEAD), tile, jnp.int32) == index
            value = jnp.where(
                of_tile,
                projected[:, h * HEAD : (h + 1) * HEAD].astype(F32),
                tx[h, place, :].astype(F32),
            )
            low = value.astype(BF16)
            emb[place, :] = low
            embT[:, place] = low.T
            queries[place, :] = (value * gain_row).astype(BF16)
            return carry

        lax.fori_loop(0, groups, body, 0)

    def score_part(h, index):
        least = max(0, index - group_reach)
        base, parts = least * GROUP, index + 1 - least
        here = pl.ds(index * GROUP, GROUP)
        query, cotangent = queries[here, :], ct[h, here, :]
        start = first[:, here] - base
        row = lax.broadcasted_iota(jnp.int32, (GROUP, GROUP), 0)
        lane = lax.broadcasted_iota(jnp.int32, (GROUP, GROUP), 1)
        scores, d_probs = [], []
        for part in range(parts):
            keys = emb[pl.ds(base + part * GROUP, GROUP), :]
            score = lax.dot_general(keys, query, NT, preferred_element_type=F32)
            d_probs.append(
                lax.dot_general(keys, cotangent, NT, preferred_element_type=F32)
            )
            allowed = row >= start - part * GROUP
            if part == parts - 1:
                allowed = allowed & (row <= lane)
            scores.append(jnp.where(allowed, score, NEG))
        highest = jnp.max(scores[0], axis=0, keepdims=True)
        for score in scores[1:]:
            highest = jnp.maximum(highest, jnp.max(score, axis=0, keepdims=True))
        total = jnp.zeros((1, GROUP), F32)
        weighted = jnp.zeros((1, GROUP), F32)
        weights = []
        for score, d_prob in zip(scores, d_probs):
            value = jnp.exp2((score - highest) * log2_scaling)
            weights.append(value)
            total = total + jnp.sum(value, axis=0, keepdims=True)
            weighted = weighted + jnp.sum(value * d_prob, axis=0, keepdims=True)
        share = 1.0 / total
        row_term = weighted * share
        scaled_share = share * scaling
        turn = index % 2
        for part, (value, d_prob) in enumerate(zip(weights, d_probs)):
            place = pl.ds(part * GROUP, GROUP)
            change = value * (d_prob - row_term)
            d_scores[turn, place, :] = (change * scaled_share).astype(BF16)
            probs[turn, place, :] = (value * share).astype(BF16)

    def product_part(h, index, gain_row):
        least = max(0, index - group_reach)
        width = (index + 1 - least) * GROUP
        band, here = pl.ds(least * GROUP, width), pl.ds(index * GROUP, GROUP)
        d_score = d_scores[index % 2, 0:width, :]
        dkv[band, :] += jnp.dot(
            d_score, queries[here, :], preferred_element_type=F32
        ) + jnp.dot(
            probs[index % 2, 0:width, :], ct[h, here, :], preferred_element_type=F32
        )
        queryT = jnp.dot(embT[:, band], d_score, preferred_element_type=F32)
        grad = queryT.T * gain_row + dkv[here, :]
        low = grad.astype(BF16).astype(F32)
        of_tile = jnp.full((GROUP, HEAD), tile, jnp.int32) == index
        send_block[h, here, :] = jnp.where(of_tile, 0.0, low).astype(BF16)
        image[...] = jnp.where(of_tile, low, image[...].astype(F32)).astype(BF16)

    def send_grads(h, least, most):
        target = out.at[
            0, :, pl.ds(pl.multiple_of(me * columns + h * HEAD, HEAD), HEAD)
        ]

        def body(step, carry):
            to = partner(step)

            @pl.when((to >= least) & (to < most))
            def _():
                pltpu.make_async_remote_copy(
                    src_ref=send_block.at[h, rows(to, BLOCK)],
                    dst_ref=target,
                    send_sem=grad_send.at[h],
                    recv_sem=grad_recv.at[h],
                    device_id=seq_id(to),
                    device_id_type=MESH,
                ).start()

            return carry

        lax.fori_loop(0, peers, body, 0)

        @pl.when((me >= least) & (me < most))
        def _():
            pltpu.make_async_copy(
                send_block.at[h, rows(me, BLOCK)], target, block_sem.at[h]
            ).start()

    def attend(h, gain_row):
        dkv[...] = jnp.zeros_like(dkv)
        image[...] = jnp.zeros_like(image)
        for index in range(groups - 1, -2, -1):
            if index >= 0:
                score_part(h, index)
            if index < groups - 1:
                product_part(h, index + 1, gain_row)
            if index in (groups // 2 - 1, -1):
                done = (index + 1) * GROUP // BLOCK
                if h == heads - 1:
                    send_grads(h, done, done + n // 2)

    def weight_term(h):
        tile_grad = image[...]

        def weight_rows(index, carry):
            mine = pl.multiple_of((2 * index + core) * out_rows, out_rows)
            theirs = pl.multiple_of((2 * index + 1 - core) * out_rows, out_rows)
            half_out[h, index] = jnp.dot(
                featT[pl.ds(theirs, out_rows), :],
                tile_grad,
                preferred_element_type=F32,
            ).astype(BF16)
            keep[index] = jnp.dot(
                featT[pl.ds(mine, out_rows), :],
                tile_grad,
                preferred_element_type=F32,
            )
            return carry

        lax.fori_loop(0, chips, weight_rows, 0)
        halves = pltpu.make_async_remote_copy(
            src_ref=half_out.at[h],
            dst_ref=half_in.at[h],
            send_sem=half_send.at[h],
            recv_sem=half_recv.at[h],
            device_id=(other_core, me),
            device_id_type=MESH,
        )
        halves.start()
        return halves

    def send_sums(h, halves):
        halves.wait()

        def add_halves(index, carry):
            value = keep[index] + half_in[h, index].astype(F32)
            keep[index] = value
            sum_out[h, index] = value.astype(BF16)
            return carry

        lax.fori_loop(0, chips, add_halves, 0)
        wgrad[:, h * HEAD : (h + 1) * HEAD] = keep[chip]

        def body(d, carry):
            to = lax.rem(chip + d, chips)
            pltpu.make_async_remote_copy(
                src_ref=sum_out.at[h, to],
                dst_ref=sum_in.at[h, d - 1],
                send_sem=sum_send.at[h],
                recv_sem=sum_recv.at[h],
                device_id=(2 * to + core, me),
                device_id_type=MESH,
            ).start()
            return carry

        lax.fori_loop(1, chips, body, 0)

    def finish(h):
        cols = slice(h * HEAD, (h + 1) * HEAD)
        await_blocks(sum_in.at[h], sum_recv.at[h])
        total = wgrad[:, cols]
        for d in range(chips - 1):
            total = total + sum_in[h, d].astype(F32)
        wgrad[:, cols] = total * (1.0 / TILE_TOK)

    for h in range(heads):
        gain_row = gain[:, h * HEAD : (h + 1) * HEAD]
        arrived = tx.at[h, pl.ds(0, peers * BLOCK)]
        await_blocks(arrived, in_recv.at[2 * h])
        prepare(h, gain_row)
        await_blocks(arrived, in_recv.at[2 * h + 1])
        if h > 0:
            send_grads(h - 1, 0, n)
        attend(h, gain_row)
        halves = weight_term(h)
        if h > 0:
            finish(h - 1)
        send_sums(h, halves)
    finish(heads - 1)

    for h in range(heads):
        sent = tx.at[h, pl.ds(0, peers * BLOCK)]
        await_blocks(sent, in_send.at[2 * h])
        await_blocks(sent, in_send.at[2 * h + 1])
        await_blocks(sum_in.at[h], sum_send.at[h])
        await_blocks(sent, grad_send.at[h])
        await_blocks(sent, grad_recv.at[h])
        own_block = send_block.at[h, pl.ds(0, BLOCK)]
        await_blocks(own_block, block_sem.at[h])
    for group in copies:
        for copy in group:
            copy.wait_send()


def per_device(
    n, enc, feat, weight, text, cot, gain, count, slot, doc
):
    heads = weight.shape[1] // HEAD
    depth = weight.shape[0]
    length = doc.shape[1]
    chips = enc // 2
    out_rows = depth // enc
    tile_rows = feat.shape[1] * n
    anywhere = pl.BlockSpec(memory_space=pl.ANY)
    hbm = pl.BlockSpec(memory_space=pltpu.HBM)
    vmem = pl.BlockSpec(memory_space=pltpu.VMEM)
    smem = pl.BlockSpec(memory_space=pltpu.SMEM)
    dma = pltpu.SemaphoreType.DMA
    ring_copies = 2 * (n // 4) + n // 2 + 2
    return pl.pallas_call(
        functools.partial(whole_kernel, n, heads, enc),
        out_shape=(
            pltpu.VMEM(text.shape, BF16),
            pltpu.VMEM((out_rows, heads * HEAD), F32),
        ),
        in_specs=[hbm] * 5 + [smem, smem, hbm],
        out_specs=(anywhere, vmem),
        scratch_shapes=[
            pltpu.VMEM((tile_rows, depth), BF16),
            pltpu.VMEM((depth, tile_rows), BF16),
            pltpu.VMEM((depth, heads * HEAD), BF16),
            pltpu.VMEM((tile_rows, heads * HEAD), BF16),
            pltpu.VMEM((heads, length, HEAD), BF16),
            pltpu.VMEM((heads, length, HEAD), BF16),
            pltpu.VMEM((length, HEAD), BF16),
            pltpu.VMEM((length, HEAD), BF16),
            pltpu.VMEM((HEAD, length), BF16),
            pltpu.VMEM((length, HEAD), F32),
            pltpu.VMEM((2, REACH + GROUP, GROUP), BF16),
            pltpu.VMEM((2, REACH + GROUP, GROUP), BF16),
            pltpu.VMEM((tile_rows, HEAD), BF16),
            pltpu.VMEM((heads, length, HEAD), BF16),
            pltpu.VMEM((1, heads * HEAD), F32),
            pltpu.VMEM((1, length), jnp.int32),
            pltpu.VMEM((1, length), jnp.int32),
            pltpu.VMEM((chips, out_rows, HEAD), F32),
            pltpu.VMEM((heads, chips, out_rows, HEAD), BF16),
            pltpu.VMEM((heads, chips, out_rows, HEAD), BF16),
            pltpu.VMEM((heads, chips, out_rows, HEAD), BF16),
            pltpu.VMEM((heads, chips - 1, out_rows, HEAD), BF16),
            dma((4 + 2 * heads,)),
            dma((ring_copies,)),
            dma((ring_copies,)),
            dma((2 * heads,)),
            dma((2 * heads,)),
            dma((heads,)),
            dma((heads,)),
            dma((heads,)),
            dma((heads,)),
            dma((heads,)),
            dma((heads,)),
            dma((heads,)),
        ],
        compiler_params=pltpu.CompilerParams(
            collective_id=0, has_side_effects=True, vmem_limit_bytes=56 * 2**20
        ),
    )(feat, weight, text, cot, gain.reshape(1, -1), count, slot, doc)


def solution(mesh):
    in_specs = (
        P("enc", "seq", None),
        P(None, "seq"),
        P("enc", "seq", None),
        P("enc", "seq", None),
        P("seq"),
        P("enc"),
        P("enc", None),
        P("enc", None),
    )
    out_specs = (P("enc", "seq", None), P("enc", "seq"))
    return jax.shard_map(
        functools.partial(per_device, mesh.shape["seq"], mesh.shape["enc"]),
        mesh=mesh,
        in_specs=in_specs,
        out_specs=out_specs,
        check_vma=False,
    )
```

```python
import functools

import jax
import jax.numpy as jnp
from jax import lax
from jax.experimental import pallas as pl
from jax.experimental.pallas import tpu as pltpu
from jax.sharding import PartitionSpec as P

HEAD = 128
TILE_TOK = 256
BLOCK = 128
GROUP = 256
REACH = 1024
DOC_VALUES = 8
NEG = -1e30
NT = (((1,), (1,)), ((), ()))
MESH = pl.DeviceIdType.MESH
F32 = jnp.float32
BF16 = jnp.bfloat16


def whole_kernel(
    n,
    heads,
    enc,
    feat,
    weight,
    text,
    cot,
    gain_in,
    count,
    slot,
    doc_in,
    out,
    wgrad,
    features,
    featT,
    wv,
    projected,
    tx,
    ct,
    queries,
    emb,
    embT,
    dkv,
    d_scores,
    probs,
    image,
    send_block,
    gain,
    doc,
    first,
    keep,
    half_out,
    half_in,
    sum_out,
    sum_in,
    local_sem,
    gather_send,
    gather_recv,
    in_send,
    in_recv,
    grad_send,
    grad_recv,
    half_send,
    half_recv,
    sum_send,
    sum_recv,
    block_sem,
):
    me = lax.axis_index("seq")
    my_enc = lax.axis_index("enc")
    core = lax.rem(my_enc, 2)
    chip = lax.div(my_enc, 2)
    chips = enc // 2
    other_core = my_enc + 1 - 2 * core
    beside = me + 1 - 2 * lax.rem(me, 2)
    columns = heads * HEAD
    shard = feat.shape[1]
    depth = feat.shape[2]
    length = n * BLOCK
    out_rows = depth // enc
    peers = n - 1

    def seq_id(index):
        return (my_enc, index)

    def along(step):
        return lax.rem(me + 2 * step + 2 * n, n)

    def partner(step):
        away = n // 2 - lax.div(step + 1, 2)
        return lax.rem(me + n + away * (1 - 2 * lax.rem(step, 2)), n)

    def rows(index, size):
        return pl.ds(pl.multiple_of(index * size, size), size)

    barrier = pltpu.get_barrier_semaphore()

    def greet_seq(d, carry):
        pl.semaphore_signal(
            barrier, inc=1, device_id=seq_id(lax.rem(me + d, n)), device_id_type=MESH
        )
        return carry

    def greet_enc(d, carry):
        to = 2 * lax.rem(chip + d, chips) + core
        pl.semaphore_signal(barrier, inc=1, device_id=(to, me), device_id_type=MESH)
        return carry

    lax.fori_loop(1, n, greet_seq, 0)
    lax.fori_loop(1, chips, greet_enc, 0)
    pl.semaphore_signal(barrier, inc=1, device_id=(other_core, me), device_id_type=MESH)

    weight_copy = pltpu.make_async_copy(weight, wv, local_sem.at[0])
    weight_copy.start()
    own_features = pltpu.make_async_copy(
        feat.at[0], features.at[rows(me, shard)], local_sem.at[1]
    )
    own_features.start()
    own = []
    for h in range(heads):
        cols = pl.ds(pl.multiple_of(me * columns + h * HEAD, HEAD), HEAD)
        own.append(
            pltpu.make_async_copy(
                text.at[0, :, cols], tx.at[h, rows(me, BLOCK)], local_sem.at[2 + 2 * h]
            )
        )
        own.append(
            pltpu.make_async_copy(
                cot.at[0, :, cols],
                ct.at[h, rows(me, BLOCK)],
                local_sem.at[3 + 2 * h],
            )
        )
    for copy in own:
        copy.start()
    gain_copy = pltpu.make_async_copy(gain_in, gain, local_sem.at[2 + 2 * heads])
    gain_copy.start()
    doc_copy = pltpu.make_async_copy(doc_in, doc, local_sem.at[3 + 2 * heads])
    doc_copy.start()

    pl.semaphore_wait(barrier, peers + chips)

    def pass_on(source, index, to, number, first_col=0, cols=depth):
        span = pl.ds(first_col, cols)
        place = features.at[rows(index, shard), span]
        return pltpu.make_async_remote_copy(
            src_ref=place if source is None else source,
            dst_ref=place,
            send_sem=gather_send.at[number],
            recv_sem=gather_recv.at[number],
            device_id=seq_id(to),
            device_id_type=MESH,
        )

    ring = n // 2
    ahead, behind = along(1), along(-1)
    full_steps = ring // 2 - 1
    half = depth // 2

    def exchange(h, source, to_cot, begin, end):
        def body(step, carry):
            to = partner(step)
            cols = pl.ds(pl.multiple_of(to * columns + h * HEAD, HEAD), HEAD)
            place = (ct if to_cot else tx).at[h, rows(me, BLOCK)]
            pltpu.make_async_remote_copy(
                src_ref=source.at[0, :, cols],
                dst_ref=place,
                send_sem=in_send.at[2 * h + to_cot],
                recv_sem=in_recv.at[2 * h + to_cot],
                device_id=seq_id(to),
                device_id_type=MESH,
            ).start()
            return carry

        lax.fori_loop(begin, end, body, 0)

    def exchange_part(h, part, parts):
        begin = peers * part // parts
        end = peers * (part + 1) // parts
        exchange(h, text, 0, begin, end)
        exchange(h, cot, 1, begin, end)

    x_base = 2 * (full_steps + 1)
    copies = []
    parts = full_steps + 1
    for step in range(full_steps):
        if step == 0:
            source = feat.at[0]
            right = pass_on(source, me, ahead, 0)
            left = pass_on(source, me, behind, full_steps + 1)
            sideways = [pass_on(source, me, beside, x_base)]
        else:
            copies[-1][0].wait_recv()
            right = pass_on(None, along(-step), ahead, step)
            copies[-1][1].wait_recv()
            left = pass_on(None, along(step), behind, full_steps + 1 + step)
            sideways = [
                pass_on(None, along(-step), beside, x_base + 2 * step - 1),
                pass_on(None, along(step), beside, x_base + 2 * step),
            ]
        for copy in [right, left] + sideways:
            copy.start()
        copies.append([right, left] + sideways)
        exchange_part(0, step, parts)
    copies[-1][0].wait_recv()
    copies[-1][1].wait_recv()
    last = full_steps
    right = pass_on(None, along(-last), ahead, last, 0, half)
    left = pass_on(None, along(last), behind, full_steps + 1 + last, half, half)
    sideways = [
        pass_on(None, along(-last), beside, x_base + 2 * last - 1),
        pass_on(None, along(last), beside, x_base + 2 * last),
    ]
    for copy in [right, left] + sideways:
        copy.start()
    exchange_part(0, full_steps, parts)
    right.wait_recv()
    left.wait_recv()
    farthest = pass_on(None, along(ring // 2), beside, x_base + 2 * last + 1)
    farthest.start()
    copies.append([right, left] + sideways + [farthest])

    for h in range(1, heads):
        exchange_part(h, 0, 1)

    doc_copy.wait()
    gain_copy.wait()
    doc_row = doc[...]
    begins = jnp.zeros_like(doc_row)
    for value in range(1, DOC_VALUES):
        below = jnp.sum((doc_row < value).astype(jnp.int32), axis=1, keepdims=True)
        begins = jnp.where(doc_row >= value, below, begins)
    first[...] = begins
    tile = jnp.where(count[0] > 0, slot[0, 0], -1)

    for group in copies:
        for copy in group[2:]:
            copy.wait_recv()
    own_features.wait()
    weight_copy.wait()

    projected[...] = jnp.dot(
        features[...], wv[...], preferred_element_type=F32
    ).astype(BF16)

    def turn_features(index, carry):
        place = rows(index, HEAD)
        featT[place, :] = features[:, place].T
        return carry

    lax.fori_loop(0, depth // HEAD, turn_features, 0)
    for copy in own:
        copy.wait()

    scaling = HEAD ** (-0.5)
    log2_scaling = scaling * 1.4426950408889634
    groups = length // GROUP
    group_reach = REACH // GROUP

    def await_blocks(like, sem):
        pltpu.make_async_copy(like, like, sem).wait()

    def prepare(h, gain_row):
        def body(index, carry):
            place = rows(index, GROUP)
            of_tile = jnp.full((GROUP, HEAD), tile, jnp.int32) == index
            value = jnp.where(
                of_tile,
                projected[:, h * HEAD : (h + 1) * HEAD].astype(F32),
                tx[h, place, :].astype(F32),
            )
            low = value.astype(BF16)
            emb[place, :] = low
            embT[:, place] = low.T
            queries[place, :] = (value * gain_row).astype(BF16)
            return carry

        lax.fori_loop(0, groups, body, 0)

    def score_part(h, index):
        least = max(0, index - group_reach)
        base, parts = least * GROUP, index + 1 - least
        here = pl.ds(index * GROUP, GROUP)
        query, cotangent = queries[here, :], ct[h, here, :]
        start = first[:, here] - base
        row = lax.broadcasted_iota(jnp.int32, (GROUP, GROUP), 0)
        lane = lax.broadcasted_iota(jnp.int32, (GROUP, GROUP), 1)
        scores, d_probs = [], []
        for part in range(parts):
            keys = emb[pl.ds(base + part * GROUP, GROUP), :]
            score = lax.dot_general(keys, query, NT, preferred_element_type=F32)
            d_probs.append(
                lax.dot_general(keys, cotangent, NT, preferred_element_type=F32)
            )
            allowed = row >= start - part * GROUP
            if part == parts - 1:
                allowed = allowed & (row <= lane)
            scores.append(jnp.where(allowed, score, NEG))
        highest = jnp.max(scores[0], axis=0, keepdims=True)
        for score in scores[1:]:
            highest = jnp.maximum(highest, jnp.max(score, axis=0, keepdims=True))
        total = jnp.zeros((1, GROUP), F32)
        weighted = jnp.zeros((1, GROUP), F32)
        weights = []
        for score, d_prob in zip(scores, d_probs):
            value = jnp.exp2((score - highest) * log2_scaling)
            weights.append(value)
            total = total + jnp.sum(value, axis=0, keepdims=True)
            weighted = weighted + jnp.sum(value * d_prob, axis=0, keepdims=True)
        share = 1.0 / total
        row_term = weighted * share
        scaled_share = share * scaling
        turn = index % 2
        for part, (value, d_prob) in enumerate(zip(weights, d_probs)):
            place = pl.ds(part * GROUP, GROUP)
            change = value * (d_prob - row_term)
            d_scores[turn, place, :] = (change * scaled_share).astype(BF16)
            probs[turn, place, :] = (value * share).astype(BF16)

    def product_part(h, index, gain_row):
        least = max(0, index - group_reach)
        width = (index + 1 - least) * GROUP
        band, here = pl.ds(least * GROUP, width), pl.ds(index * GROUP, GROUP)
        d_score = d_scores[index % 2, 0:width, :]
        dkv[band, :] += jnp.dot(
            d_score, queries[here, :], preferred_element_type=F32
        ) + jnp.dot(
            probs[index % 2, 0:width, :], ct[h, here, :], preferred_element_type=F32
        )
        queryT = jnp.dot(embT[:, band], d_score, preferred_element_type=F32)
        grad = queryT.T * gain_row + dkv[here, :]
        low = grad.astype(BF16).astype(F32)
        of_tile = jnp.full((GROUP, HEAD), tile, jnp.int32) == index
        send_block[h, here, :] = jnp.where(of_tile, 0.0, low).astype(BF16)
        image[...] = jnp.where(of_tile, low, image[...].astype(F32)).astype(BF16)

    def send_grads(h, least, most):
        target = out.at[
            0, :, pl.ds(pl.multiple_of(me * columns + h * HEAD, HEAD), HEAD)
        ]

        def body(step, carry):
            to = partner(step)

            @pl.when((to >= least) & (to < most))
            def _():
                pltpu.make_async_remote_copy(
                    src_ref=send_block.at[h, rows(to, BLOCK)],
                    dst_ref=target,
                    send_sem=grad_send.at[h],
                    recv_sem=grad_recv.at[h],
                    device_id=seq_id(to),
                    device_id_type=MESH,
                ).start()

            return carry

        lax.fori_loop(0, peers, body, 0)

        @pl.when((me >= least) & (me < most))
        def _():
            pltpu.make_async_copy(
                send_block.at[h, rows(me, BLOCK)], target, block_sem.at[h]
            ).start()

    def attend(h, gain_row):
        dkv[...] = jnp.zeros_like(dkv)
        image[...] = jnp.zeros_like(image)
        for index in range(groups - 1, -2, -1):
            if index >= 0:
                score_part(h, index)
            if index < groups - 1:
                product_part(h, index + 1, gain_row)
            if index in (groups // 2 - 1, -1):
                done = (index + 1) * GROUP // BLOCK
                if h == heads - 1:
                    send_grads(h, done, done + n // 2)

    def weight_term(h):
        tile_grad = image[...]

        def block_of_rows(index, of_core):
            place = pl.multiple_of((2 * index + of_core) * out_rows, out_rows)
            return jnp.dot(
                featT[pl.ds(place, out_rows), :], tile_grad, preferred_element_type=F32
            )

        def theirs(index, carry):
            half_out[h, index] = block_of_rows(index, 1 - core).astype(BF16)
            return carry

        def mine(index, carry):
            keep[index] = block_of_rows(index, core)
            return carry

        lax.fori_loop(0, chips, theirs, 0)
        halves = pltpu.make_async_remote_copy(
            src_ref=half_out.at[h],
            dst_ref=half_in.at[h],
            send_sem=half_send.at[h],
            recv_sem=half_recv.at[h],
            device_id=(other_core, me),
            device_id_type=MESH,
        )
        halves.start()
        lax.fori_loop(0, chips, mine, 0)
        return halves

    def send_sums(h, halves):
        halves.wait()

        wgrad[:, h * HEAD : (h + 1) * HEAD] = keep[chip] + half_in[h, chip].astype(F32)

        def body(d, carry):
            to = lax.rem(chip + d, chips)
            value = keep[to] + half_in[h, to].astype(F32)
            sum_out[h, to] = value.astype(BF16)
            pltpu.make_async_remote_copy(
                src_ref=sum_out.at[h, to],
                dst_ref=sum_in.at[h, d - 1],
                send_sem=sum_send.at[h],
                recv_sem=sum_recv.at[h],
                device_id=(2 * to + core, me),
                device_id_type=MESH,
            ).start()
            return carry

        lax.fori_loop(1, chips, body, 0)

    def finish(h):
        cols = slice(h * HEAD, (h + 1) * HEAD)
        await_blocks(sum_in.at[h], sum_recv.at[h])
        total = wgrad[:, cols]
        for d in range(chips - 1):
            total = total + sum_in[h, d].astype(F32)
        wgrad[:, cols] = total * (1.0 / TILE_TOK)

    for h in range(heads):
        gain_row = gain[:, h * HEAD : (h + 1) * HEAD]
        arrived = tx.at[h, pl.ds(0, peers * BLOCK)]
        await_blocks(arrived, in_recv.at[2 * h])
        prepare(h, gain_row)
        await_blocks(arrived, in_recv.at[2 * h + 1])
        if h > 0:
            send_grads(h - 1, 0, n)
        attend(h, gain_row)
        halves = weight_term(h)
        if h > 0:
            finish(h - 1)
        send_sums(h, halves)
    finish(heads - 1)

    for h in range(heads):
        sent = tx.at[h, pl.ds(0, peers * BLOCK)]
        await_blocks(sent, in_send.at[2 * h])
        await_blocks(sent, in_send.at[2 * h + 1])
        await_blocks(sum_in.at[h], sum_send.at[h])
        await_blocks(sent, grad_send.at[h])
        await_blocks(sent, grad_recv.at[h])
        own_block = send_block.at[h, pl.ds(0, BLOCK)]
        await_blocks(own_block, block_sem.at[h])
    for group in copies:
        for copy in group:
            copy.wait_send()


def per_device(
    n, enc, feat, weight, text, cot, gain, count, slot, doc
):
    heads = weight.shape[1] // HEAD
    depth = weight.shape[0]
    length = doc.shape[1]
    chips = enc // 2
    out_rows = depth // enc
    tile_rows = feat.shape[1] * n
    anywhere = pl.BlockSpec(memory_space=pl.ANY)
    hbm = pl.BlockSpec(memory_space=pltpu.HBM)
    vmem = pl.BlockSpec(memory_space=pltpu.VMEM)
    smem = pl.BlockSpec(memory_space=pltpu.SMEM)
    dma = pltpu.SemaphoreType.DMA
    ring_copies = 2 * (n // 4) + n // 2 + 2
    return pl.pallas_call(
        functools.partial(whole_kernel, n, heads, enc),
        out_shape=(
            pltpu.VMEM(text.shape, BF16),
            pltpu.VMEM((out_rows, heads * HEAD), F32),
        ),
        in_specs=[hbm] * 5 + [smem, smem, hbm],
        out_specs=(anywhere, vmem),
        scratch_shapes=[
            pltpu.VMEM((tile_rows, depth), BF16),
            pltpu.VMEM((depth, tile_rows), BF16),
            pltpu.VMEM((depth, heads * HEAD), BF16),
            pltpu.VMEM((tile_rows, heads * HEAD), BF16),
            pltpu.VMEM((heads, length, HEAD), BF16),
            pltpu.VMEM((heads, length, HEAD), BF16),
            pltpu.VMEM((length, HEAD), BF16),
            pltpu.VMEM((length, HEAD), BF16),
            pltpu.VMEM((HEAD, length), BF16),
            pltpu.VMEM((length, HEAD), F32),
            pltpu.VMEM((2, REACH + GROUP, GROUP), BF16),
            pltpu.VMEM((2, REACH + GROUP, GROUP), BF16),
            pltpu.VMEM((tile_rows, HEAD), BF16),
            pltpu.VMEM((heads, length, HEAD), BF16),
            pltpu.VMEM((1, heads * HEAD), F32),
            pltpu.VMEM((1, length), jnp.int32),
            pltpu.VMEM((1, length), jnp.int32),
            pltpu.VMEM((chips, out_rows, HEAD), F32),
            pltpu.VMEM((heads, chips, out_rows, HEAD), BF16),
            pltpu.VMEM((heads, chips, out_rows, HEAD), BF16),
            pltpu.VMEM((heads, chips, out_rows, HEAD), BF16),
            pltpu.VMEM((heads, chips - 1, out_rows, HEAD), BF16),
            dma((4 + 2 * heads,)),
            dma((ring_copies,)),
            dma((ring_copies,)),
            dma((2 * heads,)),
            dma((2 * heads,)),
            dma((heads,)),
            dma((heads,)),
            dma((heads,)),
            dma((heads,)),
            dma((heads,)),
            dma((heads,)),
            dma((heads,)),
        ],
        compiler_params=pltpu.CompilerParams(
            collective_id=0, has_side_effects=True, vmem_limit_bytes=56 * 2**20
        ),
    )(feat, weight, text, cot, gain.reshape(1, -1), count, slot, doc)


def solution(mesh):
    in_specs = (
        P("enc", "seq", None),
        P(None, "seq"),
        P("enc", "seq", None),
        P("enc", "seq", None),
        P("seq"),
        P("enc"),
        P("enc", None),
        P("enc", None),
    )
    out_specs = (P("enc", "seq", None), P("enc", "seq"))
    return jax.shard_map(
        functools.partial(per_device, mesh.shape["seq"], mesh.shape["enc"]),
        mesh=mesh,
        in_specs=in_specs,
        out_specs=out_specs,
        check_vma=False,
    )
```
